32 devices in a mesh: groups: 2 (over y), dom: 4 (over z), mp: 4 (over x, core).
Axes of the slice: x: 2, y: 2, z: 4, core: 2. Of those that a mesh axis runs over, the one named last changes fastest.
Arguments:
- node_latents: bfloat16 [1024, 512], P(('groups', 'dom')), parts along dimension 0, may hold values from -6 to 6
- edge_latents: bfloat16 [8192, 512], P(('groups', 'dom')), parts along dimension 0, may hold values from -6 to 6
- node_cotangent: bfloat16 [1024, 512], P(('groups', 'dom'), 'mp'), parts along dimension 0, may hold values from -6 to 6
- edge_cotangent: bfloat16 [8192, 512], P(('groups', 'dom'), 'mp'), parts along dimension 0, may hold values from -6 to 6
- senders: int32 [4096], P('dom'), may hold values from 0 to 255, as said below
- receivers: int32 [4096], P('dom'), may hold values from 0 to 127, as said below
- send_nodes: int32 [4, 4, 32], P('dom'), may hold values from 0 to 127, as said below
- edge_in_weight: bfloat16 [1536, 512], P(None, 'mp'), may hold values from -0.15625 to 0.15625
- edge_out_weight: bfloat16 [512, 512], P(None, 'mp'), may hold values from -0.25 to 0.25
- edge_gain: float32 [512], P('mp'), may hold values from 0.5 to 1.5
- node_in_weight: bfloat16 [1024, 512], P(None, 'mp'), may hold values from -0.1875 to 0.1875
- node_out_weight: bfloat16 [512, 512], P(None, 'mp'), may hold values from -0.25 to 0.25
- node_gain: float32 [512], P('mp'), may hold values from 0.5 to 1.5
Outputs:
- node_grad: bfloat16 [1024, 512], P(('groups', 'dom'), 'mp'), parts along dimension 0
- edge_grad: bfloat16 [8192, 512], P(('groups', 'dom'), 'mp'), parts along dimension 0
- edge_in_grad: float32 [3072, 512], P(('groups', 'dom'), 'mp'), parts along dimension 0
- edge_out_grad: float32 [1024, 512], P(('groups', 'dom'), 'mp'), parts along dimension 0
- edge_gain_grad: float32 [1024], P(('groups', 'mp')), parts along dimension 0
- node_in_grad: float32 [2048, 512], P(('groups', 'dom'), 'mp'), parts along dimension 0
- node_out_grad: float32 [1024, 512], P(('groups', 'dom'), 'mp'), parts along dimension 0
- node_gain_grad: float32 [1024], P(('groups', 'mp')), parts along dimension 0
The draws below stay inside these ranges and needn't reach their ends.
There are 2 independent parts, one for each index of `groups`. The reference program is written for one: setup_inputs(seed, part) draws one part's arguments, and reference() takes and returns one part's arrays. A program takes and returns all parts, laid end to end along the dimension named above; an argument that names none is the same for every part. Nothing has to cross between parts.
Inputs may be any that keep to these rules, and one draw needn't show every extreme that they name: `senders`: below 128: a node of the edge's own device. Otherwise 128 + p * 32 + k names slot k that device p fills for this device, p never the edge's own device; slots that no edge names may hold any node. `receivers`: every node receives exactly 8 of its device's edges. `send_nodes`: nodes of device p, the sender.
All inputs are finite; a program needn't handle non-finite values.
Results may differ from the reference program's by a relative error of at most 0.012.
Values may be sent and summed in bfloat16 or wider, within the bound.
A program may use at most 64 MiB of HBM per device.

```python
import jax
import jax.numpy as jnp
from jax import lax

D = 512
NODE_DEV = 128
CAP = 32
EDGE_DEV = 1024
NODES = 512
EDGES = 4096
N_DOM = 4


def crossing_counts(key):
    count_key = jax.random.fold_in(key, 11)
    counts = jax.random.randint(count_key, (N_DOM, N_DOM), 0, CAP + 1)
    source = jnp.arange(N_DOM, dtype=jnp.int32)[:, None]
    target = jnp.arange(N_DOM, dtype=jnp.int32)[None, :]
    counts = jnp.where(target == (source + 1) % N_DOM, CAP, counts)
    counts = jnp.where(source == target, 0, counts)
    return counts.astype(jnp.int32)


def draw_send_nodes(key, part):
    key = jax.random.fold_in(key, 3)
    chosen = jax.random.randint(key, (N_DOM, N_DOM, CAP), 0, NODE_DEV)
    chosen = chosen.at[0, 1 % N_DOM, 0].set(NODE_DEV - 1)
    return chosen.astype(jnp.int32)


def draw_senders(key, part):
    counts = crossing_counts(key)
    key = jax.random.fold_in(key, 5)
    key_local, key_peer, key_slot, key_cross = jax.random.split(key, 4)
    edge_owner = jnp.arange(EDGES, dtype=jnp.int32) // EDGE_DEV
    local_pick = jax.random.randint(key_local, (EDGES,), 0, NODE_DEV)
    offset = jax.random.randint(key_peer, (EDGES,), 1, N_DOM)
    peer_pick = (edge_owner + offset) % N_DOM
    filled = counts[peer_pick, edge_owner]
    fallback = (edge_owner + N_DOM - 1) % N_DOM
    peer_pick = jnp.where(filled > 0, peer_pick, fallback)
    filled = jnp.where(filled > 0, filled, CAP)
    slot_pick = jax.random.randint(key_slot, (EDGES,), 0, 1 << 20) % filled
    remote_pick = NODE_DEV + peer_pick * CAP + slot_pick
    crossing = jax.random.randint(key_cross, (EDGES,), 0, 8) < 1 + edge_owner % 4
    chosen = jnp.where(crossing, remote_pick, local_pick)
    chosen = chosen.at[0].set(NODE_DEV + (N_DOM - 1) * CAP + CAP - 1)
    return chosen.astype(jnp.int32)


def draw_receivers(key, part):
    key = jax.random.fold_in(key, 7)
    base_row = jnp.tile(jnp.arange(NODE_DEV, dtype=jnp.int32), EDGE_DEV // NODE_DEV)
    device_keys = jax.random.split(key, N_DOM)
    shuffled = jax.vmap(lambda one_key: jax.random.permutation(one_key, base_row))(device_keys)
    return shuffled.reshape(EDGES).astype(jnp.int32)


def block_scale(key, shape, shards, low, top_value):
    loudness, own = 1.0, jax.random.fold_in(key, 6)
    for dim, blocks in shards:
        heights = jnp.exp(jax.random.uniform(jax.random.fold_in(own, dim), (blocks,), jnp.float32, low / len(shards), top_value / len(shards)))
        loudness = loudness * jnp.repeat(heights, shape[dim] // blocks).reshape([-1 if axis == dim else 1 for axis in range(len(shape))])
    return loudness


def noise(stream_key, dims, scale, bound, cuts=(), held_as=jnp.bfloat16):
    drawn = jax.random.normal(stream_key, dims, jnp.float32) * scale
    if len(cuts) > 0:
        drawn = block_scale(stream_key, dims, cuts, -0.22, 0.18) * drawn
    return jnp.clip(drawn, min=-bound, max=bound).astype(held_as)


def setup_inputs(seed: int = 0, part: int = 0) -> dict:
    seeds = jax.random.split(jax.random.key(seed), 14)
    part_splits = jax.random.split(jax.random.fold_in(seeds[13], part), 14)
    node_latents = noise(part_splits[0], (NODES, D), 1.0, 6.0, ((0, 4),))
    edge_latents = noise(part_splits[1], (EDGES, D), 1.0, 6.0, ((0, 4),))
    node_cotangent = noise(part_splits[2], (NODES, D), 1.0, 6.0, ((0, 4), (1, 4)))
    edge_cotangent = noise(part_splits[3], (EDGES, D), 1.0, 6.0, ((0, 4), (1, 4)))
    senders = draw_senders(jax.random.fold_in(seeds[13], 71), part)
    receivers = draw_receivers(jax.random.fold_in(seeds[13], 71), part)
    send_nodes = draw_send_nodes(jax.random.fold_in(seeds[13], 71), part)
    edge_in_weight = noise(seeds[7], (3 * D, D), (3 * D) ** -0.5, 0.15625, ((1, 4),))
    edge_out_weight = noise(seeds[8], (D, D), D ** -0.5, 0.25, ((1, 4),))
    edge_gain = jnp.clip(1.0 + 0.1 * jax.random.normal(seeds[9], (D,), jnp.float32), 0.5, 1.5)
    node_in_weight = noise(seeds[10], (2 * D, D), (2 * D) ** -0.5, 0.1875, ((1, 4),))
    node_out_weight = noise(seeds[11], (D, D), D ** -0.5, 0.25, ((1, 4),))
    node_gain = jnp.clip(1.0 + 0.1 * jax.random.normal(seeds[12], (D,), jnp.float32), 0.5, 1.5)
    return {"node_latents": node_latents, "edge_latents": edge_latents, "node_cotangent": node_cotangent, "edge_cotangent": edge_cotangent, "senders": senders, "receivers": receivers, "send_nodes": send_nodes, "edge_in_weight": edge_in_weight, "edge_out_weight": edge_out_weight, "edge_gain": edge_gain, "node_in_weight": node_in_weight, "node_out_weight": node_out_weight, "node_gain": node_gain}


norm_eps = 1e-05

def silu_slope(values):
    sigma = jax.nn.sigmoid(values)
    return sigma * (1.0 + values * (1.0 - sigma))

def norm_parts(values):
    center = lax.optimization_barrier(jnp.mean(values, axis=-1, keepdims=True))
    spread = lax.optimization_barrier(jnp.mean(values * values, axis=-1, keepdims=True)) - center * center
    scale_inv = lax.rsqrt(spread + norm_eps)
    return ((values - center) * scale_inv, scale_inv)

def norm_back(upstream, gain_row, hatted, scale_inv):
    weighted = upstream * gain_row
    first_mean = lax.optimization_barrier(jnp.mean(weighted, axis=-1, keepdims=True))
    second_mean = lax.optimization_barrier(jnp.mean(weighted * hatted, axis=-1, keepdims=True))
    return scale_inv * (weighted - first_mean - hatted * second_mean)

def dot_first(left, right):
    return lax.dot_general(left, right, (((0,), (0,)), ((), ())), preferred_element_type=jnp.float32)

def dot_last(left, right):
    return lax.dot_general(left, right, (((1,), (1,)), ((), ())), preferred_element_type=jnp.float32)

def reference(node_latents, edge_latents, node_cotangent, edge_cotangent, senders, receivers, send_nodes, edge_in_weight, edge_out_weight, edge_gain, node_in_weight, node_out_weight, node_gain):
    edge_owner = (jnp.arange(EDGES, dtype=jnp.int32) // EDGE_DEV).astype(jnp.int32)
    is_local = senders < NODE_DEV
    slot_index = jnp.maximum(senders - NODE_DEV, 0).astype(jnp.int32)
    peer_index = (slot_index // CAP).astype(jnp.int32)
    slot_rank = (slot_index % CAP).astype(jnp.int32)
    remote_node = send_nodes[peer_index, edge_owner, slot_rank]
    sender_node = jnp.where(is_local, edge_owner * NODE_DEV + senders, peer_index * NODE_DEV + remote_node).astype(jnp.int32)
    receiver_node = (edge_owner * NODE_DEV + receivers).astype(jnp.int32)
    edge_input = jnp.concatenate([edge_latents, node_latents[sender_node], node_latents[receiver_node]], axis=1)
    edge_pre = jnp.dot(edge_input, edge_in_weight, preferred_element_type=jnp.float32)
    edge_hidden = jax.nn.silu(edge_pre).astype(jnp.bfloat16)
    edge_out = jnp.dot(edge_hidden, edge_out_weight, preferred_element_type=jnp.float32)
    edge_hat, edge_rstd = norm_parts(edge_out)
    edge_update = (edge_hat * edge_gain).astype(jnp.bfloat16)
    aggregate = jax.ops.segment_sum(edge_update.astype(jnp.float32), receiver_node, num_segments=NODES).astype(jnp.bfloat16)
    node_input = jnp.concatenate([node_latents, aggregate], axis=1)
    node_pre = jnp.dot(node_input, node_in_weight, preferred_element_type=jnp.float32)
    node_hidden = jax.nn.silu(node_pre).astype(jnp.bfloat16)
    node_out = jnp.dot(node_hidden, node_out_weight, preferred_element_type=jnp.float32)
    node_hat, node_rstd = norm_parts(node_out)
    edge_scale = float(EDGES) ** (-0.5)
    node_scale = float(NODES) ** (-0.5)
    node_cot = node_cotangent.astype(jnp.float32)
    edge_cot = edge_cotangent.astype(jnp.float32)
    node_gain_grad = lax.optimization_barrier(jnp.sum(node_cot * node_hat, axis=0)) * node_scale
    node_slope = norm_back(node_cot, node_gain, node_hat, node_rstd).astype(jnp.bfloat16)
    node_out_grad = dot_first(node_hidden, node_slope) * node_scale
    node_delta = (dot_last(node_slope, node_out_weight) * silu_slope(node_pre)).astype(jnp.bfloat16)
    node_in_grad = dot_first(node_input, node_delta) * node_scale
    node_back = dot_last(node_delta, node_in_weight)
    update_grad = edge_cot + node_back[:, D:][receiver_node]
    edge_gain_grad = lax.optimization_barrier(jnp.sum(update_grad * edge_hat, axis=0)) * edge_scale
    edge_slope = norm_back(update_grad, edge_gain, edge_hat, edge_rstd).astype(jnp.bfloat16)
    edge_out_grad = dot_first(edge_hidden, edge_slope) * edge_scale
    edge_delta = (dot_last(edge_slope, edge_out_weight) * silu_slope(edge_pre)).astype(jnp.bfloat16)
    edge_in_grad = dot_first(edge_input, edge_delta) * edge_scale
    edge_back = dot_last(edge_delta, edge_in_weight)
    edge_grad = (edge_cot + edge_back[:, :D]).astype(jnp.bfloat16)
    sender_part = edge_back[:, D:2 * D]
    receiver_part = edge_back[:, 2 * D:]
    local_sums = jax.ops.segment_sum(jnp.where(is_local[:, None], sender_part, 0.0), sender_node, num_segments=NODES)
    crossing_key = (edge_owner * (N_DOM * CAP) + slot_index).astype(jnp.int32)
    crossing_sums = jax.ops.segment_sum(jnp.where(is_local[:, None], 0.0, sender_part), crossing_key, num_segments=N_DOM * N_DOM * CAP).astype(jnp.bfloat16)
    crossing_sums = lax.optimization_barrier(crossing_sums).astype(jnp.float32)
    dest_index = jnp.arange(N_DOM, dtype=jnp.int32)[:, None, None] + jnp.zeros((N_DOM, N_DOM, CAP), jnp.int32)
    peer_grid = jnp.arange(N_DOM, dtype=jnp.int32)[None, :, None] + jnp.zeros((N_DOM, N_DOM, CAP), jnp.int32)
    rank_grid = jnp.arange(CAP, dtype=jnp.int32)[None, None, :] + jnp.zeros((N_DOM, N_DOM, CAP), jnp.int32)
    target_node = (peer_grid * NODE_DEV + send_nodes[peer_grid, dest_index, rank_grid]).reshape(-1).astype(jnp.int32)
    returned = jax.ops.segment_sum(crossing_sums, target_node, num_segments=NODES)
    receiver_sums = jax.ops.segment_sum(receiver_part, receiver_node, num_segments=NODES)
    node_grad = (node_cot + node_back[:, :D] + receiver_sums + local_sums + returned).astype(jnp.bfloat16)
    return (node_grad, edge_grad, edge_in_grad, edge_out_grad, edge_gain_grad, node_in_grad, node_out_grad, node_gain_grad)
```

```python
import functools

import jax
import jax.numpy as jnp
from jax import lax
from jax.experimental import pallas as pl
from jax.experimental.pallas import tpu as pltpu
from jax.sharding import PartitionSpec as P

norm_eps = 1e-05


def shortened(value):

    def short(part):
        return part.astype(jnp.bfloat16) if part.dtype == jnp.float32 else part

    return jax.tree.map(short, value)


def silu_slope(values):
    sigma = jax.nn.sigmoid(values)
    return sigma * (1.0 + values * (1.0 - sigma))


def dot_first(left, right):
    return lax.dot_general(
        left, right, (((0,), (0,)), ((), ())), preferred_element_type=jnp.float32
    )


def dot_last(left, right):
    return lax.dot_general(
        left, right, (((1,), (1,)), ((), ())), preferred_element_type=jnp.float32
    )


def add_rows_into(index, count, values):
    table = (index[:, None] == jnp.arange(count, dtype=jnp.int32)[None, :]).astype(values.dtype)
    if values.dtype == jnp.float32:
        return lax.dot_general(
            table,
            values,
            (((0,), (0,)), ((), ())),
            precision=lax.Precision.HIGHEST,
            preferred_element_type=jnp.float32,
        )
    return dot_first(table, values)


def join_columns(values):
    return jax.tree.map(
        lambda part, own: part.astype(own.dtype),
        lax.all_gather(shortened(values), "mp", axis=1, tiled=True),
        values,
    )


def row_moments(first_term, second_term):
    return lax.psum((jnp.sum(first_term, axis=1), jnp.sum(second_term, axis=1)), "mp")


def swap_crossing(values):
    return lax.all_to_all(values, "dom", split_axis=0, concat_axis=0, tiled=True)


def reduce_grads(values):
    return (
        lax.psum_scatter(
            values[0].astype(jnp.bfloat16), "dom", scatter_dimension=0, tiled=True
        ).astype(jnp.float32),
        lax.psum_scatter(
            values[1].astype(jnp.bfloat16), "dom", scatter_dimension=0, tiled=True
        ).astype(jnp.float32),
    )


def norm_parts(values, latent_width):
    first_sum, second_sum = row_moments(values, values * values)
    center = (first_sum / latent_width)[:, None]
    spread = (second_sum / latent_width)[:, None] - center * center
    scale_inv = lax.rsqrt(spread + norm_eps)
    return ((values - center) * scale_inv, scale_inv)


def norm_back(upstream, gain_row, hatted, scale_inv, latent_width):
    weighted = upstream * gain_row
    first_sum, second_sum = row_moments(weighted, weighted * hatted)
    return scale_inv * (
        weighted
        - (first_sum / latent_width)[:, None]
        - hatted * (second_sum / latent_width)[:, None]
    )


def body(
    node_latents,
    edge_latents,
    node_cotangent,
    edge_cotangent,
    senders,
    receivers,
    send_nodes,
    edge_in_weight,
    edge_out_weight,
    edge_gain,
    node_in_weight,
    node_out_weight,
    node_gain,
):
    dom_count = lax.axis_size("dom")
    mp_count = lax.axis_size("mp")
    nodes_dev, latent_width = node_latents.shape
    edges_dev = edge_latents.shape[0]
    column_share = latent_width // mp_count
    column_start = lax.axis_index("mp") * column_share
    edge_scale = float(edges_dev * dom_count) ** (-0.5)
    node_scale = float(nodes_dev * dom_count) ** (-0.5)
    send_table = send_nodes[0].reshape(-1)
    halo_rows = swap_crossing(node_latents[send_table])
    extended = jnp.concatenate([node_latents, halo_rows], axis=0)
    edge_input = jnp.concatenate([edge_latents, extended[senders], node_latents[receivers]], axis=1)
    edge_pre = jnp.dot(edge_input, edge_in_weight, preferred_element_type=jnp.float32)
    edge_hidden = join_columns(jax.nn.silu(edge_pre).astype(jnp.bfloat16))
    edge_out = jnp.dot(edge_hidden, edge_out_weight, preferred_element_type=jnp.float32)
    edge_hat, edge_rstd = norm_parts(edge_out, latent_width)
    edge_update = (edge_hat * edge_gain).astype(jnp.bfloat16)
    aggregate = add_rows_into(receivers, nodes_dev, edge_update).astype(jnp.bfloat16)
    node_input = jnp.concatenate([node_latents, join_columns(aggregate)], axis=1)
    node_pre = jnp.dot(node_input, node_in_weight, preferred_element_type=jnp.float32)
    node_hidden = join_columns(jax.nn.silu(node_pre).astype(jnp.bfloat16))
    node_out = jnp.dot(node_hidden, node_out_weight, preferred_element_type=jnp.float32)
    node_hat, node_rstd = norm_parts(node_out, latent_width)
    out_edge_full, out_node_full = join_columns((edge_out_weight, node_out_weight))
    in_edge_full, in_node_full = join_columns((edge_in_weight, node_in_weight))
    node_cot = node_cotangent.astype(jnp.float32)
    edge_cot = edge_cotangent.astype(jnp.float32)
    node_gain_part = jnp.sum(node_cot * node_hat, axis=0) * node_scale
    node_slope = norm_back(node_cot, node_gain, node_hat, node_rstd, latent_width).astype(
        jnp.bfloat16
    )
    node_out_part = dot_first(node_hidden, node_slope) * node_scale
    node_slope_full = join_columns(node_slope)
    node_hidden_rows = lax.dynamic_slice_in_dim(out_node_full, column_start, column_share, 0)
    node_delta = (dot_last(node_slope_full, node_hidden_rows) * silu_slope(node_pre)).astype(
        jnp.bfloat16
    )
    node_in_part = dot_first(node_input, node_delta) * node_scale
    node_in_grad, node_out_grad = reduce_grads((node_in_part, node_out_part))
    node_delta_full = join_columns(node_delta)
    node_feature_rows = lax.dynamic_slice_in_dim(
        in_node_full.reshape(2, latent_width, latent_width), column_start, column_share, 1
    )
    node_back = jnp.einsum(
        "nj,bkj->bnk", node_delta_full, node_feature_rows, preferred_element_type=jnp.float32
    )
    update_grad = edge_cot + node_back[1][receivers]
    edge_gain_part = jnp.sum(update_grad * edge_hat, axis=0) * edge_scale
    edge_slope = norm_back(update_grad, edge_gain, edge_hat, edge_rstd, latent_width).astype(
        jnp.bfloat16
    )
    edge_out_part = dot_first(edge_hidden, edge_slope) * edge_scale
    edge_slope_full = join_columns(edge_slope)
    edge_hidden_rows = lax.dynamic_slice_in_dim(out_edge_full, column_start, column_share, 0)
    edge_delta = (dot_last(edge_slope_full, edge_hidden_rows) * silu_slope(edge_pre)).astype(
        jnp.bfloat16
    )
    edge_in_part = dot_first(edge_input, edge_delta) * edge_scale
    edge_delta_full = join_columns(edge_delta)
    edge_feature_rows = lax.dynamic_slice_in_dim(
        in_edge_full.reshape(3, latent_width, latent_width), column_start, column_share, 1
    )
    edge_back = jnp.einsum(
        "ej,bkj->bek", edge_delta_full, edge_feature_rows, preferred_element_type=jnp.float32
    )
    edge_grad = (edge_cot + edge_back[0]).astype(jnp.bfloat16)
    sender_sums = add_rows_into(senders, nodes_dev + send_table.shape[0], edge_back[1])
    returned_rows = swap_crossing(sender_sums[nodes_dev:].astype(jnp.bfloat16))
    returned = add_rows_into(send_table, nodes_dev, returned_rows)
    receiver_sums = add_rows_into(receivers, nodes_dev, edge_back[2])
    node_grad = (
        node_cot + node_back[0] + receiver_sums + sender_sums[:nodes_dev] + returned
    ).astype(jnp.bfloat16)
    edge_in_grad, edge_out_grad = reduce_grads((edge_in_part, edge_out_part))
    edge_gain_grad, node_gain_grad = lax.psum((edge_gain_part, node_gain_part), "dom")
    return (
        node_grad,
        edge_grad,
        edge_in_grad,
        edge_out_grad,
        edge_gain_grad,
        node_in_grad,
        node_out_grad,
        node_gain_grad,
    )


def dot_plain(left, right):
    return jnp.dot(left, right, preferred_element_type=jnp.float32)


def two_terms(values):
    high = values.astype(jnp.bfloat16)
    low = (values - high.astype(jnp.float32)).astype(jnp.bfloat16)
    return jnp.concatenate([high, low], axis=1)


def join_terms(values):
    half = values.shape[1] // 2
    return values[:, :half] + values[:, half:]


def repeat_rows(values, times):
    rows, columns = values.shape
    return jnp.broadcast_to(values[:, None, :], (rows, times, columns)).reshape(
        rows * times, columns
    )


def sum_rows(values, times):
    rows, columns = values.shape
    return jnp.sum(values.reshape(rows // times, times, columns), axis=1)


def local_norm(values):
    center = jnp.mean(values, axis=1, keepdims=True)
    spread = jnp.mean(values * values, axis=1, keepdims=True) - center * center
    scale_inv = lax.rsqrt(spread + norm_eps)
    return (values - center) * scale_inv, scale_inv


def local_norm_back(upstream, gain_row, hatted, scale_inv):
    weighted = upstream * gain_row
    first_mean = jnp.mean(weighted, axis=1, keepdims=True)
    second_mean = jnp.mean(weighted * hatted, axis=1, keepdims=True)
    return scale_inv * (weighted - first_mean - hatted * second_mean)


def fused_kernel(
    dom,
    mp,
    degree,
    nodes,
    edges,
    node_cot,
    edge_cot,
    senders,
    receivers,
    table,
    w_in,
    w_out,
    e_gain,
    nw_in,
    nw_out,
    n_gain,
    node_grad,
    edge_grad,
    edge_in_grad,
    edge_out_grad,
    edge_gain_grad,
    node_in_grad,
    node_out_grad,
    node_gain_grad,
    halo_send,
    extended,
    w_out_all,
    nw_in_all,
    nw_out_all,
    w_in_rows,
    e_gain_all,
    n_gain_all,
    perm,
    edges_sorted,
    cot_sorted,
    grad_sorted,
    sender_hot,
    pre_cols,
    pre_rows,
    cot_rows,
    ncot_rows,
    agg_all,
    nhid_all,
    ndelta_all,
    nslope_own,
    nslope_cols,
    delta_all,
    gain_part,
    gain_recv,
    gain_sum,
    gain_dom,
    eo_part,
    eo_recv,
    eo_send,
    eo_dom,
    ei_send,
    ei_dom,
    no_send,
    no_dom,
    ni_send,
    ni_dom,
    cross_send,
    cross_recv,
    back_terms,
    receiver_back,
    mp_send_sem,
    mp_recv_sem,
    dom_send_sem,
    dom_recv_sem,
):
    f32, bf16 = jnp.float32, jnp.bfloat16
    node_count, width = nodes.shape
    edge_count = edges.shape[0]
    share = width // mp
    my_nodes, my_edges = node_count // mp, edge_count // mp
    slots = table.shape[1]
    cap = slots // dom
    edge_scale = float(edge_count * dom) ** (-0.5)
    node_scale = float(node_count * dom) ** (-0.5)
    me_m, me_d = lax.axis_index("mp"), lax.axis_index("dom")

    def rows(index, size):
        return pl.ds(pl.multiple_of(index * size, size), size)

    mp_to = [lax.rem(me_m + k, mp) for k in range(1, mp)]
    mp_from = [lax.rem(me_m + mp - k, mp) for k in range(1, mp)]
    dom_to = [lax.rem(me_d + k, dom) for k in range(1, dom)]
    dom_from = [lax.rem(me_d + dom - k, dom) for k in range(1, dom)]
    started = []

    def push(axis, kind, peers, source, target):
        send, recv = (
            (mp_send_sem, mp_recv_sem) if axis == "mp" else (dom_send_sem, dom_recv_sem)
        )
        copies = []
        for k, peer in enumerate(peers):
            copy = pltpu.make_async_remote_copy(
                src_ref=source(peer),
                dst_ref=target,
                send_sem=send.at[kind, k],
                recv_sem=recv.at[kind, k],
                device_id={axis: peer},
                device_id_type=pl.DeviceIdType.MESH,
            )
            copy.start()
            copies.append(copy)
        started.extend(copies)
        return copies

    def arrived(copies):
        for copy in copies:
            copy.wait_recv()

    barrier = pltpu.get_barrier_semaphore()
    for axis, peers in (("mp", mp_to), ("dom", dom_to)):
        for peer in peers:
            pl.semaphore_signal(
                barrier, inc=1, device_id={axis: peer}, device_id_type=pl.DeviceIdType.MESH
            )

    table_hot = (
        lax.broadcasted_iota(jnp.int32, (node_count, slots), 0) == table[...]
    ).astype(bf16)
    halo_send[...] = dot_first(table_hot, nodes[...]).astype(bf16)
    extended[pl.ds(0, node_count), :] = nodes[...]
    extended[pl.ds(pl.multiple_of(node_count + me_d * cap, cap), cap), :] = jnp.zeros(
        (cap, width), bf16
    )
    pl.semaphore_wait(barrier, mp + dom - 2)

    halo = push(
        "dom",
        0,
        dom_to,
        lambda peer: halo_send.at[rows(peer, cap), :],
        extended.at[pl.ds(pl.multiple_of(node_count + me_d * cap, cap), cap), :],
    )
    own_cols = rows(me_m, share)
    w_out_in = push("mp", 0, mp_to, lambda peer: w_out, w_out_all.at[:, own_cols])
    gain_in = push("mp", 1, mp_to, lambda peer: e_gain, e_gain_all.at[:, own_cols])
    ngain_in = push("mp", 2, mp_to, lambda peer: n_gain, n_gain_all.at[:, own_cols])
    ncot_in = push(
        "mp", 3, mp_to, lambda peer: node_cot.at[rows(peer, my_nodes), :], ncot_rows.at[:, own_cols]
    )
    w_out_all[:, own_cols] = w_out[...]
    e_gain_all[:, own_cols] = e_gain[...]
    n_gain_all[:, own_cols] = n_gain[...]
    ncot_rows[:, own_cols] = node_cot[rows(me_m, my_nodes), :]
    nw_in_all[:, own_cols] = nw_in[...]
    nw_out_all[:, own_cols] = nw_out[...]
    w_in_rows[:, :, own_cols] = w_in[:, rows(me_m, share), :]

    lane = 128
    before = (
        lax.broadcasted_iota(jnp.int32, (lane, lane), 0)
        < lax.broadcasted_iota(jnp.int32, (lane, lane), 1)
    ).astype(bf16)
    offset = jnp.zeros((node_count, 1), f32)
    places = []
    for start in range(0, edge_count, lane):
        received = receivers[:, start : start + lane]
        hot = lax.broadcasted_iota(jnp.int32, (node_count, lane), 0) == received
        hot32 = hot.astype(f32)
        earlier = dot_plain(hot32.astype(bf16), before) + offset
        rank = jnp.sum(hot32 * earlier, axis=0, keepdims=True)
        places.append(received * degree + rank.astype(jnp.int32))
        offset = offset + jnp.sum(hot32, axis=1, keepdims=True)
    place = jnp.concatenate(places, axis=1)
    sender_cols = (
        lax.broadcasted_iota(jnp.int32, (node_count + slots, edge_count), 0) == senders[...]
    ).astype(bf16)
    receiver_pre = dot_plain(nodes[...], w_in[2])
    for part in range(mp):
        block = pl.ds(part * my_edges, my_edges)
        hot = (
            lax.broadcasted_iota(jnp.int32, (my_edges, edge_count), 0) + part * my_edges == place
        ).astype(bf16)
        perm[block, :] = hot
        edges_sorted[block, :] = dot_plain(hot, edges[...]).astype(bf16)
        cot_sorted[block, :] = dot_plain(hot, edge_cot[...]).astype(bf16)
        sender_hot[block, :] = dot_last(hot, sender_cols).astype(bf16)
    arrived(halo)
    sender_pre = two_terms(dot_plain(extended[...], w_in[1]))
    for part in range(mp):
        block = pl.ds(part * my_edges, my_edges)
        local = dot_plain(edges_sorted[block, :], w_in[0])
        local = local + repeat_rows(
            receiver_pre[part * my_nodes : (part + 1) * my_nodes], degree
        )
        local = local + join_terms(dot_plain(sender_hot[block, :], sender_pre))
        pre_cols[block, :] = local.astype(bf16)
    pre_in = push(
        "mp", 4, mp_to, lambda peer: pre_cols.at[rows(peer, my_edges), :], pre_rows.at[:, own_cols]
    )
    nw_in_in = push("mp", 6, mp_to, lambda peer: nw_in, nw_in_all.at[:, own_cols])
    nw_out_in = push("mp", 7, mp_to, lambda peer: nw_out, nw_out_all.at[:, own_cols])
    cot_in = push(
        "mp", 5, mp_to, lambda peer: cot_sorted.at[rows(peer, my_edges), :], cot_rows.at[:, own_cols]
    )
    w_in_in = push(
        "mp", 8, mp_to, lambda peer: w_in.at[:, rows(peer, share), :], w_in_rows.at[:, :, own_cols]
    )
    pre_rows[:, own_cols] = pre_cols[rows(me_m, my_edges), :]
    cot_rows[:, own_cols] = cot_sorted[rows(me_m, my_edges), :]

    arrived(pre_in)
    edge_pre = pre_rows[...].astype(f32)
    edge_hidden = (edge_pre * jax.nn.sigmoid(edge_pre)).astype(bf16)
    arrived(w_out_in)
    edge_out = dot_plain(edge_hidden, w_out_all[...])
    edge_hat, edge_rstd = local_norm(edge_out)
    arrived(gain_in)
    edge_update = (edge_hat * e_gain_all[...]).astype(bf16).astype(f32)
    own_rows = rows(me_m, my_nodes)
    aggregate = sum_rows(edge_update, degree).astype(bf16)
    agg_all[own_rows, :] = aggregate
    agg_in = push(
        "mp", 9, mp_to, lambda peer: agg_all.at[own_rows, :], agg_all.at[own_rows, :]
    )
    arrived(nw_in_in)
    node_pre = dot_plain(nodes[own_rows, :], nw_in_all[pl.ds(0, width), :]) + dot_plain(
        aggregate, nw_in_all[pl.ds(width, width), :]
    )
    node_hidden = (node_pre * jax.nn.sigmoid(node_pre)).astype(bf16)
    nhid_all[own_rows, :] = node_hidden
    nhid_in = push(
        "mp", 10, mp_to, lambda peer: nhid_all.at[own_rows, :], nhid_all.at[own_rows, :]
    )
    arrived(nw_out_in)
    node_hat, node_rstd = local_norm(dot_plain(node_hidden, nw_out_all[...]))
    arrived(ncot_in)
    arrived(ngain_in)
    ncot = ncot_rows[...].astype(f32)
    gain_part[...] = jnp.zeros_like(gain_part)
    gain_part[0:1, :] = jnp.sum(ncot * node_hat, axis=0, keepdims=True) * node_scale
    node_slope = local_norm_back(ncot, n_gain_all[...], node_hat, node_rstd).astype(bf16)
    nslope_own[...] = node_slope
    nslope_in = push(
        "mp", 11, mp_to, lambda peer: nslope_own.at[:, rows(peer, share)], nslope_cols.at[own_rows, :]
    )
    nslope_cols[own_rows, :] = nslope_own[:, own_cols]
    node_delta = (dot_last(node_slope, nw_out_all[...]) * silu_slope(node_pre)).astype(bf16)
    ndelta_all[own_rows, :] = node_delta
    ndelta_in = push(
        "mp", 12, mp_to, lambda peer: ndelta_all.at[own_rows, :], ndelta_all.at[own_rows, :]
    )
    agg_back = dot_last(node_delta, nw_in_all[pl.ds(width, width), :])
    arrived(cot_in)
    update_grad = cot_rows[...].astype(f32) + repeat_rows(agg_back, degree)
    gain_part[1:2, :] = jnp.sum(update_grad * edge_hat, axis=0, keepdims=True) * edge_scale
    edge_slope = local_norm_back(update_grad, e_gain_all[...], edge_hat, edge_rstd).astype(bf16)
    edge_pre = pre_rows[...].astype(f32)
    edge_delta = (dot_last(edge_slope, w_out_all[...]) * silu_slope(edge_pre)).astype(bf16)
    own_edges = rows(me_m, my_edges)
    delta_all[own_edges, :] = edge_delta
    delta_in = push(
        "mp", 13, mp_to, lambda peer: delta_all.at[own_edges, :], delta_all.at[own_edges, :]
    )
    eo_part[...] = (dot_first(edge_hidden, edge_slope) * edge_scale).astype(bf16)
    eo_in = push("mp", 14, mp_to, lambda peer: eo_part.at[:, rows(peer, share)], eo_recv.at[me_m])
    gain_part_in = push(
        "mp", 15, mp_to, lambda peer: gain_part.at[:, rows(peer, share)], gain_recv.at[me_m]
    )
    eo_recv[me_m] = eo_part[:, own_cols]
    gain_recv[me_m] = gain_part[:, own_cols]

    arrived(agg_in)
    arrived(nhid_in)
    arrived(nslope_in)
    arrived(ndelta_in)
    no_send[...] = (dot_first(nhid_all[...], nslope_cols[...]) * node_scale).astype(bf16)
    ndelta_cols = ndelta_all[:, own_cols]
    ni_send[pl.ds(0, width), :] = (dot_first(nodes[...], ndelta_cols) * node_scale).astype(bf16)
    ni_send[pl.ds(width, width), :] = (dot_first(agg_all[...], ndelta_cols) * node_scale).astype(
        bf16
    )

    def scatter_sum(kind, parts, landed):
        size = landed.shape[1]
        copies = push(
            "dom", kind, dom_to, lambda peer: parts.at[rows(peer, size), :], landed.at[me_d]
        )
        landed[me_d] = parts[rows(me_d, size), :]
        return copies

    no_in = scatter_sum(1, no_send, no_dom)
    ni_in = scatter_sum(2, ni_send, ni_dom)
    total = node_cot[...].astype(f32) + dot_last(ndelta_all[...], nw_in_all[own_cols, :])

    arrived(w_in_in)

    def input_back(owner):
        block = rows(owner, my_edges)
        deltas = delta_all[block, :]
        grad = cot_sorted[block, :].astype(f32) + dot_last(deltas, w_in_rows[0])
        grad_sorted[block, :] = grad.astype(bf16)
        back_terms[block, :] = two_terms(dot_last(deltas, w_in_rows[1]))
        receiver_back[rows(owner, my_nodes), :] = sum_rows(
            dot_last(deltas, w_in_rows[2]), degree
        )

    input_back(me_m)
    for copy, owner in zip(delta_in, mp_from):
        copy.wait_recv()
        input_back(owner)
    sender_sums = join_terms(dot_first(sender_hot[...], back_terms[...]))
    cross_send[...] = sender_sums[node_count:].astype(bf16)
    cross_recv[rows(me_d, cap), :] = jnp.zeros((cap, share), bf16)
    cross_in = push(
        "dom",
        3,
        dom_to,
        lambda peer: cross_send.at[rows(peer, cap), :],
        cross_recv.at[rows(me_d, cap), :],
    )
    delta_cols = delta_all[:, own_cols]
    own_scale = jnp.float32(edge_scale)
    ei_send[pl.ds(0, width), :] = (dot_first(edges_sorted[...], delta_cols) * own_scale).astype(
        bf16
    )
    by_sender = two_terms(dot_first(sender_hot[...], delta_cols))
    ei_send[pl.ds(width, width), :] = (
        join_terms(dot_first(extended[...], by_sender)) * own_scale
    ).astype(bf16)
    by_receiver = two_terms(sum_rows(delta_cols.astype(f32), degree))
    ei_send[pl.ds(2 * width, width), :] = (
        join_terms(dot_first(nodes[...], by_receiver)) * own_scale
    ).astype(bf16)
    ei_in = scatter_sum(4, ei_send, ei_dom)
    arrived(eo_in)
    eo_send[...] = jnp.sum(eo_recv[...].astype(f32), axis=0).astype(bf16)
    eo_out = scatter_sum(5, eo_send, eo_dom)
    arrived(gain_part_in)
    gain_sum[...] = jnp.sum(gain_recv[...], axis=0)
    gain_out = push("dom", 6, dom_to, lambda peer: gain_sum, gain_dom.at[me_d])
    gain_dom[me_d] = gain_sum[...]

    edge_grad[...] = dot_first(perm[...], grad_sorted[...]).astype(bf16)
    arrived(no_in)
    node_out_grad[...] = jnp.sum(no_dom[...].astype(f32), axis=0)
    arrived(ni_in)
    node_in_grad[...] = jnp.sum(ni_dom[...].astype(f32), axis=0)
    arrived(cross_in)
    node_grad[...] = (
        total + receiver_back[...] + sender_sums[:node_count] + dot_plain(table_hot, cross_recv[...])
    ).astype(bf16)
    arrived(gain_out)
    gains = jnp.sum(gain_dom[...], axis=0)
    node_gain_grad[...] = gains[0:1]
    edge_gain_grad[...] = gains[1:2]
    arrived(eo_out)
    edge_out_grad[...] = jnp.sum(eo_dom[...].astype(f32), axis=0)
    arrived(ei_in)
    edge_in_grad[...] = jnp.sum(ei_dom[...].astype(f32), axis=0)
    for copy in started:
        copy.wait_send()


def fits_kernel(mesh):
    return mesh.shape["dom"] * mesh.shape["mp"] <= 16


def fused_body(
    node_latents,
    edge_latents,
    node_cotangent,
    edge_cotangent,
    senders,
    receivers,
    send_nodes,
    edge_in_weight,
    edge_out_weight,
    edge_gain,
    node_in_weight,
    node_out_weight,
    node_gain,
):
    dom, mp = lax.axis_size("dom"), lax.axis_size("mp")
    node_count, width = node_latents.shape
    edge_count = edge_latents.shape[0]
    slots = send_nodes.shape[1] * send_nodes.shape[2]
    share = width // mp
    my_nodes, my_edges = node_count // mp, edge_count // mp
    f32, bf16 = jnp.float32, jnp.bfloat16
    shape = jax.ShapeDtypeStruct
    outs = (
        shape((node_count, share), bf16),
        shape((edge_count, share), bf16),
        shape((3 * width // dom, share), f32),
        shape((width // dom, share), f32),
        shape((1, share), f32),
        shape((2 * width // dom, share), f32),
        shape((width // dom, share), f32),
        shape((1, share), f32),
    )
    scratch = [
        ((slots, width), bf16),
        ((node_count + slots, width), bf16),
        ((width, width), bf16),
        ((2 * width, width), bf16),
        ((width, width), bf16),
        ((3, share, width), bf16),
        ((1, width), f32),
        ((1, width), f32),
        ((edge_count, edge_count), bf16),
        ((edge_count, width), bf16),
        ((edge_count, share), bf16),
        ((edge_count, share), bf16),
        ((edge_count, node_count + slots), bf16),
        ((edge_count, share), bf16),
        ((my_edges, width), bf16),
        ((my_edges, width), bf16),
        ((my_nodes, width), bf16),
        ((node_count, width), bf16),
        ((node_count, width), bf16),
        ((node_count, width), bf16),
        ((my_nodes, width), bf16),
        ((node_count, share), bf16),
        ((edge_count, width), bf16),
        ((8, width), f32),
        ((mp, 8, share), f32),
        ((8, share), f32),
        ((dom, 8, share), f32),
        ((width, width), bf16),
        ((mp, width, share), bf16),
        ((width, share), bf16),
        ((dom, width // dom, share), bf16),
        ((3 * width, share), bf16),
        ((dom, 3 * width // dom, share), bf16),
        ((width, share), bf16),
        ((dom, width // dom, share), bf16),
        ((2 * width, share), bf16),
        ((dom, 2 * width // dom, share), bf16),
        ((slots, share), bf16),
        ((slots, share), bf16),
        ((edge_count, 2 * share), bf16),
        ((node_count, share), f32),
    ]
    vmem = pl.BlockSpec(memory_space=pltpu.VMEM)
    results = pl.pallas_call(
        functools.partial(fused_kernel, dom, mp, edge_count // node_count),
        out_shape=outs,
        in_specs=[vmem] * 13,
        out_specs=tuple([vmem] * 8),
        scratch_shapes=[pltpu.VMEM(dims, kind) for dims, kind in scratch]
        + [
            pltpu.SemaphoreType.DMA((16, mp - 1)),
            pltpu.SemaphoreType.DMA((16, mp - 1)),
            pltpu.SemaphoreType.DMA((7, dom - 1)),
            pltpu.SemaphoreType.DMA((7, dom - 1)),
        ],
        compiler_params=pltpu.CompilerParams(
            collective_id=0, has_side_effects=True, vmem_limit_bytes=56 * 1024 * 1024
        ),
        name="layer_backward",
    )(
        node_latents,
        edge_latents,
        node_cotangent,
        edge_cotangent,
        senders.reshape(1, edge_count),
        receivers.reshape(1, edge_count),
        send_nodes.reshape(1, slots),
        edge_in_weight.reshape(3, width, share),
        edge_out_weight,
        edge_gain.reshape(1, share),
        node_in_weight,
        node_out_weight,
        node_gain.reshape(1, share),
    )
    results = list(results)
    results[4], results[7] = results[4].reshape(share), results[7].reshape(share)
    return tuple(results)


def solution(mesh):
    in_specs = (
        P(("groups", "dom"), None),
        P(("groups", "dom"), None),
        P(("groups", "dom"), "mp"),
        P(("groups", "dom"), "mp"),
        P("dom"),
        P("dom"),
        P("dom", None, None),
        P(None, "mp"),
        P(None, "mp"),
        P("mp"),
        P(None, "mp"),
        P(None, "mp"),
        P("mp"),
    )
    out_specs = (
        P(("groups", "dom"), "mp"),
        P(("groups", "dom"), "mp"),
        P(("groups", "dom"), "mp"),
        P(("groups", "dom"), "mp"),
        P(("groups", "mp")),
        P(("groups", "dom"), "mp"),
        P(("groups", "dom"), "mp"),
        P(("groups", "mp")),
    )
    return jax.shard_map(fused_body if fits_kernel(mesh) else body, mesh=mesh, in_specs=in_specs, out_specs=out_specs, check_vma=False)
```

```python
import functools

import jax
import jax.numpy as jnp
from jax import lax
from jax.experimental import pallas as pl
from jax.experimental.pallas import tpu as pltpu
from jax.sharding import PartitionSpec as P

norm_eps = 1e-05


def shortened(value):

    def short(part):
        return part.astype(jnp.bfloat16) if part.dtype == jnp.float32 else part

    return jax.tree.map(short, value)


def silu_slope(values):
    sigma = jax.nn.sigmoid(values)
    return sigma * (1.0 + values * (1.0 - sigma))


def dot_first(left, right):
    return lax.dot_general(
        left, right, (((0,), (0,)), ((), ())), preferred_element_type=jnp.float32
    )


def dot_last(left, right):
    return lax.dot_general(
        left, right, (((1,), (1,)), ((), ())), preferred_element_type=jnp.float32
    )


def add_rows_into(index, count, values):
    table = (index[:, None] == jnp.arange(count, dtype=jnp.int32)[None, :]).astype(values.dtype)
    if values.dtype == jnp.float32:
        return lax.dot_general(
            table,
            values,
            (((0,), (0,)), ((), ())),
            precision=lax.Precision.HIGHEST,
            preferred_element_type=jnp.float32,
        )
    return dot_first(table, values)


def join_columns(values):
    return jax.tree.map(
        lambda part, own: part.astype(own.dtype),
        lax.all_gather(shortened(values), "mp", axis=1, tiled=True),
        values,
    )


def row_moments(first_term, second_term):
    return lax.psum((jnp.sum(first_term, axis=1), jnp.sum(second_term, axis=1)), "mp")


def swap_crossing(values):
    return lax.all_to_all(values, "dom", split_axis=0, concat_axis=0, tiled=True)


def reduce_grads(values):
    return (
        lax.psum_scatter(
            values[0].astype(jnp.bfloat16), "dom", scatter_dimension=0, tiled=True
        ).astype(jnp.float32),
        lax.psum_scatter(
            values[1].astype(jnp.bfloat16), "dom", scatter_dimension=0, tiled=True
        ).astype(jnp.float32),
    )


def norm_parts(values, latent_width):
    first_sum, second_sum = row_moments(values, values * values)
    center = (first_sum / latent_width)[:, None]
    spread = (second_sum / latent_width)[:, None] - center * center
    scale_inv = lax.rsqrt(spread + norm_eps)
    return ((values - center) * scale_inv, scale_inv)


def norm_back(upstream, gain_row, hatted, scale_inv, latent_width):
    weighted = upstream * gain_row
    first_sum, second_sum = row_moments(weighted, weighted * hatted)
    return scale_inv * (
        weighted
        - (first_sum / latent_width)[:, None]
        - hatted * (second_sum / latent_width)[:, None]
    )


def body(
    node_latents,
    edge_latents,
    node_cotangent,
    edge_cotangent,
    senders,
    receivers,
    send_nodes,
    edge_in_weight,
    edge_out_weight,
    edge_gain,
    node_in_weight,
    node_out_weight,
    node_gain,
):
    dom_count = lax.axis_size("dom")
    mp_count = lax.axis_size("mp")
    nodes_dev, latent_width = node_latents.shape
    edges_dev = edge_latents.shape[0]
    column_share = latent_width // mp_count
    column_start = lax.axis_index("mp") * column_share
    edge_scale = float(edges_dev * dom_count) ** (-0.5)
    node_scale = float(nodes_dev * dom_count) ** (-0.5)
    send_table = send_nodes[0].reshape(-1)
    halo_rows = swap_crossing(node_latents[send_table])
    extended = jnp.concatenate([node_latents, halo_rows], axis=0)
    edge_input = jnp.concatenate([edge_latents, extended[senders], node_latents[receivers]], axis=1)
    edge_pre = jnp.dot(edge_input, edge_in_weight, preferred_element_type=jnp.float32)
    edge_hidden = join_columns(jax.nn.silu(edge_pre).astype(jnp.bfloat16))
    edge_out = jnp.dot(edge_hidden, edge_out_weight, preferred_element_type=jnp.float32)
    edge_hat, edge_rstd = norm_parts(edge_out, latent_width)
    edge_update = (edge_hat * edge_gain).astype(jnp.bfloat16)
    aggregate = add_rows_into(receivers, nodes_dev, edge_update).astype(jnp.bfloat16)
    node_input = jnp.concatenate([node_latents, join_columns(aggregate)], axis=1)
    node_pre = jnp.dot(node_input, node_in_weight, preferred_element_type=jnp.float32)
    node_hidden = join_columns(jax.nn.silu(node_pre).astype(jnp.bfloat16))
    node_out = jnp.dot(node_hidden, node_out_weight, preferred_element_type=jnp.float32)
    node_hat, node_rstd = norm_parts(node_out, latent_width)
    out_edge_full, out_node_full = join_columns((edge_out_weight, node_out_weight))
    in_edge_full, in_node_full = join_columns((edge_in_weight, node_in_weight))
    node_cot = node_cotangent.astype(jnp.float32)
    edge_cot = edge_cotangent.astype(jnp.float32)
    node_gain_part = jnp.sum(node_cot * node_hat, axis=0) * node_scale
    node_slope = norm_back(node_cot, node_gain, node_hat, node_rstd, latent_width).astype(
        jnp.bfloat16
    )
    node_out_part = dot_first(node_hidden, node_slope) * node_scale
    node_slope_full = join_columns(node_slope)
    node_hidden_rows = lax.dynamic_slice_in_dim(out_node_full, column_start, column_share, 0)
    node_delta = (dot_last(node_slope_full, node_hidden_rows) * silu_slope(node_pre)).astype(
        jnp.bfloat16
    )
    node_in_part = dot_first(node_input, node_delta) * node_scale
    node_in_grad, node_out_grad = reduce_grads((node_in_part, node_out_part))
    node_delta_full = join_columns(node_delta)
    node_feature_rows = lax.dynamic_slice_in_dim(
        in_node_full.reshape(2, latent_width, latent_width), column_start, column_share, 1
    )
    node_back = jnp.einsum(
        "nj,bkj->bnk", node_delta_full, node_feature_rows, preferred_element_type=jnp.float32
    )
    update_grad = edge_cot + node_back[1][receivers]
    edge_gain_part = jnp.sum(update_grad * edge_hat, axis=0) * edge_scale
    edge_slope = norm_back(update_grad, edge_gain, edge_hat, edge_rstd, latent_width).astype(
        jnp.bfloat16
    )
    edge_out_part = dot_first(edge_hidden, edge_slope) * edge_scale
    edge_slope_full = join_columns(edge_slope)
    edge_hidden_rows = lax.dynamic_slice_in_dim(out_edge_full, column_start, column_share, 0)
    edge_delta = (dot_last(edge_slope_full, edge_hidden_rows) * silu_slope(edge_pre)).astype(
        jnp.bfloat16
    )
    edge_in_part = dot_first(edge_input, edge_delta) * edge_scale
    edge_delta_full = join_columns(edge_delta)
    edge_feature_rows = lax.dynamic_slice_in_dim(
        in_edge_full.reshape(3, latent_width, latent_width), column_start, column_share, 1
    )
    edge_back = jnp.einsum(
        "ej,bkj->bek", edge_delta_full, edge_feature_rows, preferred_element_type=jnp.float32
    )
    edge_grad = (edge_cot + edge_back[0]).astype(jnp.bfloat16)
    sender_sums = add_rows_into(senders, nodes_dev + send_table.shape[0], edge_back[1])
    returned_rows = swap_crossing(sender_sums[nodes_dev:].astype(jnp.bfloat16))
    returned = add_rows_into(send_table, nodes_dev, returned_rows)
    receiver_sums = add_rows_into(receivers, nodes_dev, edge_back[2])
    node_grad = (
        node_cot + node_back[0] + receiver_sums + sender_sums[:nodes_dev] + returned
    ).astype(jnp.bfloat16)
    edge_in_grad, edge_out_grad = reduce_grads((edge_in_part, edge_out_part))
    edge_gain_grad, node_gain_grad = lax.psum((edge_gain_part, node_gain_part), "dom")
    return (
        node_grad,
        edge_grad,
        edge_in_grad,
        edge_out_grad,
        edge_gain_grad,
        node_in_grad,
        node_out_grad,
        node_gain_grad,
    )


def dot_plain(left, right):
    return jnp.dot(left, right, preferred_element_type=jnp.float32)


def two_terms(values):
    high = values.astype(jnp.bfloat16)
    low = (values - high.astype(jnp.float32)).astype(jnp.bfloat16)
    return jnp.concatenate([high, low], axis=1)


def join_terms(values):
    half = values.shape[1] // 2
    return values[:, :half] + values[:, half:]


def repeat_rows(values, times):
    rows, columns = values.shape
    return jnp.broadcast_to(values[:, None, :], (rows, times, columns)).reshape(
        rows * times, columns
    )


def sum_rows(values, times):
    rows, columns = values.shape
    return jnp.sum(values.reshape(rows // times, times, columns), axis=1)


def local_norm(values):
    center = jnp.mean(values, axis=1, keepdims=True)
    spread = jnp.mean(values * values, axis=1, keepdims=True) - center * center
    scale_inv = lax.rsqrt(spread + norm_eps)
    return (values - center) * scale_inv, scale_inv


def local_norm_back(upstream, gain_row, hatted, scale_inv):
    weighted = upstream * gain_row
    first_mean = jnp.mean(weighted, axis=1, keepdims=True)
    second_mean = jnp.mean(weighted * hatted, axis=1, keepdims=True)
    return scale_inv * (weighted - first_mean - hatted * second_mean)


def fused_kernel(
    dom,
    mp,
    degree,
    nodes,
    edges,
    node_cot,
    edge_cot,
    senders,
    receivers,
    table,
    w_in,
    w_out,
    e_gain,
    nw_in,
    nw_out,
    n_gain,
    node_grad,
    edge_grad,
    edge_in_grad,
    edge_out_grad,
    edge_gain_grad,
    node_in_grad,
    node_out_grad,
    node_gain_grad,
    halo_send,
    extended,
    w_out_all,
    nw_in_all,
    nw_out_all,
    w_in_rows,
    e_gain_all,
    n_gain_all,
    perm,
    edges_sorted,
    cot_sorted,
    grad_sorted,
    sender_hot,
    pre_cols,
    pre_rows,
    cot_rows,
    ncot_rows,
    agg_all,
    nhid_all,
    ndelta_all,
    nslope_own,
    nslope_cols,
    delta_all,
    gain_part,
    gain_recv,
    gain_sum,
    gain_dom,
    eo_part,
    eo_recv,
    eo_send,
    eo_dom,
    ei_send,
    ei_dom,
    no_send,
    no_dom,
    ni_send,
    ni_dom,
    cross_send,
    cross_recv,
    back_terms,
    receiver_back,
    mp_send_sem,
    mp_recv_sem,
    dom_send_sem,
    dom_recv_sem,
    one_send_sem,
    one_recv_sem,
):
    f32, bf16 = jnp.float32, jnp.bfloat16
    node_count, width = nodes.shape
    edge_count = edges.shape[0]
    share = width // mp
    my_nodes, my_edges = node_count // mp, edge_count // mp
    cap = table.shape[1]
    slots = dom * cap
    edge_scale = float(edge_count * dom) ** (-0.5)
    node_scale = float(node_count * dom) ** (-0.5)
    me_m, me_d = lax.axis_index("mp"), lax.axis_index("dom")

    def rows(index, size):
        return pl.ds(pl.multiple_of(index * size, size), size)

    me_g = lax.axis_index("groups")
    mate = me_m + 1 - 2 * lax.rem(me_m, 2)
    across = lax.rem(me_m + 2, mp)
    across_mate = lax.rem(mate + 2, mp)
    mp_to = [lax.rem(me_m + k, mp) for k in range(1, mp)]
    mp_from = [lax.rem(me_m + mp - k, mp) for k in range(1, mp)]
    dom_to = [lax.rem(me_d + k, dom) for k in range(1, dom)]
    dom_from = [lax.rem(me_d + dom - k, dom) for k in range(1, dom)]
    started = []

    def push(axis, kind, peers, source, target):
        send, recv = (
            (mp_send_sem, mp_recv_sem) if axis == "mp" else (dom_send_sem, dom_recv_sem)
        )
        copies = []
        for k, peer in enumerate(peers):
            copy = pltpu.make_async_remote_copy(
                src_ref=source(peer),
                dst_ref=target,
                send_sem=send.at[kind, k],
                recv_sem=recv.at[kind, k],
                device_id={axis: peer},
                device_id_type=pl.DeviceIdType.MESH,
            )
            copy.start()
            copies.append(copy)
        started.extend(copies)
        return copies

    used = iter(range(one_send_sem.shape[0]))

    def put(device, source, target):
        slot = next(used)
        copy = pltpu.make_async_remote_copy(
            src_ref=source,
            dst_ref=target,
            send_sem=one_send_sem.at[slot],
            recv_sem=one_recv_sem.at[slot],
            device_id=device,
            device_id_type=pl.DeviceIdType.MESH,
        )
        copy.start()
        started.append(copy)
        return copy

    def arrived(copies):
        for copy in copies:
            copy.wait_recv()

    barrier = pltpu.get_barrier_semaphore()
    for axis, peers in (("mp", mp_to), ("dom", dom_to), ("groups", [1 - me_g])):
        for peer in peers:
            pl.semaphore_signal(
                barrier, inc=1, device_id={axis: peer}, device_id_type=pl.DeviceIdType.MESH
            )

    table_row = jnp.concatenate([table[p : p + 1, :] for p in range(dom)], axis=1)
    table_hot = (
        lax.broadcasted_iota(jnp.int32, (node_count, slots), 0) == table_row
    ).astype(bf16)
    halo_send[...] = dot_first(table_hot, nodes[...]).astype(bf16)
    extended[pl.ds(0, node_count), :] = nodes[...]
    extended[pl.ds(pl.multiple_of(node_count + me_d * cap, cap), cap), :] = jnp.zeros(
        (cap, width), bf16
    )
    pl.semaphore_wait(barrier, mp + dom - 1)

    halo = push(
        "dom",
        0,
        dom_to,
        lambda peer: halo_send.at[rows(peer, cap), :],
        extended.at[pl.ds(pl.multiple_of(node_count + me_d * cap, cap), cap), :],
    )
    own_cols = rows(me_m, share)
    across_cols = rows(across, share)

    def weight_first(weight, whole):
        half = rows(me_g, weight.shape[0] // 2)
        return [
            put({"mp": across}, weight.at[half, :], whole.at[half, own_cols]),
            put({"mp": mate}, weight, whole.at[:, own_cols]),
        ]

    def weight_second(first, whole):
        first[0].wait_recv()
        part = whole.at[rows(me_g, whole.shape[0] // 2), across_cols]
        return first[1:] + [
            put({"groups": 1 - me_g}, part, part),
            put({"mp": mate}, part, part),
        ]

    def weight_third(second, whole):
        second[1].wait_recv()
        part = whole.at[rows(1 - me_g, whole.shape[0] // 2), across_cols]
        return [second[0], second[2], put({"mp": mate}, part, part)]

    w_out_in = weight_first(w_out, w_out_all)
    nw_in_in = weight_first(nw_in, nw_in_all)
    nw_out_in = weight_first(nw_out, nw_out_all)
    gain_in = push("mp", 1, mp_to, lambda peer: e_gain, e_gain_all.at[:, own_cols])
    ngain_in = push("mp", 2, mp_to, lambda peer: n_gain, n_gain_all.at[:, own_cols])
    ncot_in = push(
        "mp", 3, mp_to, lambda peer: node_cot.at[rows(peer, my_nodes), :], ncot_rows.at[:, own_cols]
    )
    w_out_all[:, own_cols] = w_out[...]
    e_gain_all[:, own_cols] = e_gain[...]
    n_gain_all[:, own_cols] = n_gain[...]
    ncot_rows[:, own_cols] = node_cot[rows(me_m, my_nodes), :]
    nw_in_all[:, own_cols] = nw_in[...]
    nw_out_all[:, own_cols] = nw_out[...]
    w_in_rows[:, :, own_cols] = w_in[:, rows(me_m, share), :]

    lane = 128
    before = (
        lax.broadcasted_iota(jnp.int32, (lane, lane), 0)
        < lax.broadcasted_iota(jnp.int32, (lane, lane), 1)
    ).astype(bf16)
    offset = jnp.zeros((node_count, 1), f32)
    places = []
    for start in range(0, edge_count, lane):
        received = receivers[:, start : start + lane]
        hot = lax.broadcasted_iota(jnp.int32, (node_count, lane), 0) == received
        hot32 = hot.astype(f32)
        earlier = dot_plain(hot32.astype(bf16), before) + offset
        rank = jnp.sum(hot32 * earlier, axis=0, keepdims=True)
        places.append(received * degree + rank.astype(jnp.int32))
        offset = offset + jnp.sum(hot32, axis=1, keepdims=True)
    place = jnp.concatenate(places, axis=1)
    sender_cols = (
        lax.broadcasted_iota(jnp.int32, (node_count + slots, edge_count), 0) == senders[...]
    ).astype(bf16)
    receiver_pre = dot_plain(nodes[...], w_in[2])
    for part in range(mp):
        block = pl.ds(part * my_edges, my_edges)
        hot = (
            lax.broadcasted_iota(jnp.int32, (my_edges, edge_count), 0) + part * my_edges == place
        ).astype(bf16)
        perm[block, :] = hot
        edges_sorted[block, :] = dot_plain(hot, edges[...]).astype(bf16)
        cot_sorted[block, :] = dot_plain(hot, edge_cot[...]).astype(bf16)
        sender_hot[block, :] = dot_last(hot, sender_cols).astype(bf16)
        if part == mp // 2:
            w_out_in = weight_second(w_out_in, w_out_all)
    nw_in_in = weight_second(nw_in_in, nw_in_all)
    nw_out_in = weight_second(nw_out_in, nw_out_all)
    arrived(halo)
    sender_pre = two_terms(dot_plain(extended[...], w_in[1]))
    for part in range(mp):
        block = pl.ds(part * my_edges, my_edges)
        local = dot_plain(edges_sorted[block, :], w_in[0])
        local = local + repeat_rows(
            receiver_pre[part * my_nodes : (part + 1) * my_nodes], degree
        )
        local = local + join_terms(dot_plain(sender_hot[block, :], sender_pre))
        pre_cols[block, :] = local.astype(bf16)
    pre_in = push(
        "mp", 4, mp_to, lambda peer: pre_cols.at[rows(peer, my_edges), :], pre_rows.at[:, own_cols]
    )
    cot_in = push(
        "mp", 5, mp_to, lambda peer: cot_sorted.at[rows(peer, my_edges), :], cot_rows.at[:, own_cols]
    )
    w_in_in = push(
        "mp", 8, mp_to, lambda peer: w_in.at[:, rows(peer, share), :], w_in_rows.at[:, :, own_cols]
    )
    pre_rows[:, own_cols] = pre_cols[rows(me_m, my_edges), :]
    cot_rows[:, own_cols] = cot_sorted[rows(me_m, my_edges), :]

    w_out_in = weight_third(w_out_in, w_out_all)
    arrived(pre_in)
    edge_pre = pre_rows[...].astype(f32)
    edge_hidden = (edge_pre * jax.nn.sigmoid(edge_pre)).astype(bf16)
    arrived(w_out_in)
    edge_out = dot_plain(edge_hidden, w_out_all[...])
    edge_hat, edge_rstd = local_norm(edge_out)
    arrived(gain_in)
    edge_update = (edge_hat * e_gain_all[...]).astype(bf16).astype(f32)
    own_rows = rows(me_m, my_nodes)
    aggregate = sum_rows(edge_update, degree).astype(bf16)
    agg_all[own_rows, :] = aggregate
    agg_in = push(
        "mp", 9, mp_to, lambda peer: agg_all.at[own_rows, :], agg_all.at[own_rows, :]
    )
    nw_in_in = weight_third(nw_in_in, nw_in_all)
    nw_out_in = weight_third(nw_out_in, nw_out_all)
    arrived(nw_in_in)
    node_pre = dot_plain(nodes[own_rows, :], nw_in_all[pl.ds(0, width), :]) + dot_plain(
        aggregate, nw_in_all[pl.ds(width, width), :]
    )
    node_hidden = (node_pre * jax.nn.sigmoid(node_pre)).astype(bf16)
    nhid_all[own_rows, :] = node_hidden
    nhid_in = push(
        "mp", 10, mp_to, lambda peer: nhid_all.at[own_rows, :], nhid_all.at[own_rows, :]
    )
    arrived(nw_out_in)
    node_hat, node_rstd = local_norm(dot_plain(node_hidden, nw_out_all[...]))
    arrived(ncot_in)
    arrived(ngain_in)
    ncot = ncot_rows[...].astype(f32)
    gain_part[...] = jnp.zeros_like(gain_part)
    gain_part[0:1, :] = jnp.sum(ncot * node_hat, axis=0, keepdims=True) * node_scale
    node_slope = local_norm_back(ncot, n_gain_all[...], node_hat, node_rstd).astype(bf16)
    nslope_own[...] = node_slope
    nslope_in = push(
        "mp", 11, mp_to, lambda peer: nslope_own.at[:, rows(peer, share)], nslope_cols.at[own_rows, :]
    )
    nslope_cols[own_rows, :] = nslope_own[:, own_cols]
    node_delta = (dot_last(node_slope, nw_out_all[...]) * silu_slope(node_pre)).astype(bf16)
    ndelta_all[own_rows, :] = node_delta
    ndelta_in = push(
        "mp", 12, mp_to, lambda peer: ndelta_all.at[own_rows, :], ndelta_all.at[own_rows, :]
    )
    agg_back = dot_last(node_delta, nw_in_all[pl.ds(width, width), :])
    arrived(cot_in)
    update_grad = cot_rows[...].astype(f32) + repeat_rows(agg_back, degree)
    gain_part[1:2, :] = jnp.sum(update_grad * edge_hat, axis=0, keepdims=True) * edge_scale
    edge_slope = local_norm_back(update_grad, e_gain_all[...], edge_hat, edge_rstd).astype(bf16)
    edge_pre = pre_rows[...].astype(f32)
    edge_delta = (dot_last(edge_slope, w_out_all[...]) * silu_slope(edge_pre)).astype(bf16)
    own_edges = rows(me_m, my_edges)
    delta_all[own_edges, :] = edge_delta
    own_delta = delta_all.at[own_edges, :]
    delta_across = put({"mp": across}, own_delta, own_delta)
    delta_mate = put({"mp": mate}, own_delta, own_delta)
    eo_part[...] = (dot_first(edge_hidden, edge_slope) * edge_scale).astype(bf16)
    eo_in = [
        put({"mp": mate}, eo_part.at[:, rows(mate, share)], eo_recv.at[0]),
        put({"mp": mate}, eo_part.at[:, rows(across_mate, share)], eo_recv.at[1]),
    ]
    gain_part_in = push(
        "mp", 15, mp_to, lambda peer: gain_part.at[:, rows(peer, share)], gain_recv.at[me_m]
    )
    gain_recv[me_m] = gain_part[:, own_cols]

    arrived(eo_in)
    eo_recv[2] = (eo_part[:, across_cols].astype(f32) + eo_recv[1].astype(f32)).astype(bf16)
    eo_across = put({"mp": across}, eo_recv.at[2], eo_recv.at[3])

    arrived(agg_in)
    arrived(nhid_in)
    arrived(nslope_in)
    arrived(ndelta_in)
    no_send[...] = (dot_first(nhid_all[...], nslope_cols[...]) * node_scale).astype(bf16)
    ndelta_cols = ndelta_all[:, own_cols]
    ni_send[pl.ds(0, width), :] = (dot_first(nodes[...], ndelta_cols) * node_scale).astype(bf16)
    ni_send[pl.ds(width, width), :] = (dot_first(agg_all[...], ndelta_cols) * node_scale).astype(
        bf16
    )

    def scatter_sum(kind, parts, landed):
        size = landed.shape[1]
        copies = push(
            "dom", kind, dom_to, lambda peer: parts.at[rows(peer, size), :], landed.at[me_d]
        )
        landed[me_d] = parts[rows(me_d, size), :]
        return copies

    no_in = scatter_sum(1, no_send, no_dom)
    ni_in = scatter_sum(2, ni_send, ni_dom)
    total = node_cot[...].astype(f32) + dot_last(ndelta_all[...], nw_in_all[own_cols, :])

    arrived(w_in_in)

    def input_back(owner):
        block = rows(owner, my_edges)
        deltas = delta_all[block, :]
        grad = cot_sorted[block, :].astype(f32) + dot_last(deltas, w_in_rows[0])
        grad_sorted[block, :] = grad.astype(bf16)
        back_terms[block, :] = two_terms(dot_last(deltas, w_in_rows[1]))
        receiver_back[rows(owner, my_nodes), :] = sum_rows(
            dot_last(deltas, w_in_rows[2]), degree
        )

    input_back(me_m)
    delta_mate.wait_recv()
    delta_across.wait_recv()
    across_delta = delta_all.at[rows(across, my_edges), :]
    delta_last = put({"mp": mate}, across_delta, across_delta)
    input_back(mate)
    input_back(across)
    delta_last.wait_recv()
    input_back(across_mate)
    sender_sums = join_terms(dot_first(sender_hot[...], back_terms[...]))
    cross_send[...] = sender_sums[node_count:].astype(bf16)
    cross_recv[rows(me_d, cap), :] = jnp.zeros((cap, share), bf16)
    cross_in = push(
        "dom",
        3,
        dom_to,
        lambda peer: cross_send.at[rows(peer, cap), :],
        cross_recv.at[rows(me_d, cap), :],
    )
    delta_cols = delta_all[:, own_cols]
    own_scale = jnp.float32(edge_scale)
    ei_send[pl.ds(0, width), :] = (dot_first(edges_sorted[...], delta_cols) * own_scale).astype(
        bf16
    )
    by_sender = two_terms(dot_first(sender_hot[...], delta_cols))
    ei_send[pl.ds(width, width), :] = (
        join_terms(dot_first(extended[...], by_sender)) * own_scale
    ).astype(bf16)
    by_receiver = two_terms(sum_rows(delta_cols.astype(f32), degree))
    ei_send[pl.ds(2 * width, width), :] = (
        join_terms(dot_first(nodes[...], by_receiver)) * own_scale
    ).astype(bf16)
    ei_in = scatter_sum(4, ei_send, ei_dom)
    eo_across.wait_recv()
    eo_send[...] = (
        eo_part[:, own_cols].astype(f32) + eo_recv[0].astype(f32) + eo_recv[3].astype(f32)
    ).astype(bf16)
    eo_out = scatter_sum(5, eo_send, eo_dom)
    arrived(gain_part_in)
    gain_sum[...] = jnp.sum(gain_recv[...], axis=0)
    gain_out = push("dom", 6, dom_to, lambda peer: gain_sum, gain_dom.at[me_d])
    gain_dom[me_d] = gain_sum[...]

    edge_grad[...] = dot_first(perm[...], grad_sorted[...]).astype(bf16)
    arrived(no_in)
    node_out_grad[...] = jnp.sum(no_dom[...].astype(f32), axis=0)
    arrived(ni_in)
    node_in_grad[...] = jnp.sum(ni_dom[...].astype(f32), axis=0)
    arrived(cross_in)
    node_grad[...] = (
        total + receiver_back[...] + sender_sums[:node_count] + dot_plain(table_hot, cross_recv[...])
    ).astype(bf16)
    arrived(gain_out)
    gains = jnp.sum(gain_dom[...], axis=0)
    node_gain_grad[...] = gains[0:1]
    edge_gain_grad[...] = gains[1:2]
    arrived(eo_out)
    edge_out_grad[...] = jnp.sum(eo_dom[...].astype(f32), axis=0)
    arrived(ei_in)
    edge_in_grad[...] = jnp.sum(ei_dom[...].astype(f32), axis=0)
    for copy in started:
        copy.wait_send()


def fits_kernel(mesh):
    return mesh.shape["groups"] == 2 and mesh.shape["mp"] == 4 and mesh.shape["dom"] <= 8


def hand_over_kernel(*refs):
    count = len(refs) // 2
    sems = refs[-1]
    copies = [
        pltpu.make_async_copy(refs[k], refs[count + k], sems.at[k]) for k in range(count)
    ]
    for copy in copies:
        copy.start()
    for copy in copies:
        copy.wait()


def fused_body(
    node_latents,
    edge_latents,
    node_cotangent,
    edge_cotangent,
    senders,
    receivers,
    send_nodes,
    edge_in_weight,
    edge_out_weight,
    edge_gain,
    node_in_weight,
    node_out_weight,
    node_gain,
):
    dom, mp = lax.axis_size("dom"), lax.axis_size("mp")
    node_count, width = node_latents.shape
    edge_count = edge_latents.shape[0]
    slots = send_nodes.shape[1] * send_nodes.shape[2]
    share = width // mp
    my_nodes, my_edges = node_count // mp, edge_count // mp
    f32, bf16 = jnp.float32, jnp.bfloat16
    shape = jax.ShapeDtypeStruct
    outs = (
        shape((node_count, share), bf16),
        shape((edge_count, share), bf16),
        shape((3 * width // dom, share), f32),
        shape((width // dom, share), f32),
        shape((1, share), f32),
        shape((2 * width // dom, share), f32),
        shape((width // dom, share), f32),
        shape((1, share), f32),
    )
    scratch = [
        ((slots, width), bf16),
        ((node_count + slots, width), bf16),
        ((width, width), bf16),
        ((2 * width, width), bf16),
        ((width, width), bf16),
        ((3, share, width), bf16),
        ((1, width), f32),
        ((1, width), f32),
        ((edge_count, edge_count), bf16),
        ((edge_count, width), bf16),
        ((edge_count, share), bf16),
        ((edge_count, share), bf16),
        ((edge_count, node_count + slots), bf16),
        ((edge_count, share), bf16),
        ((my_edges, width), bf16),
        ((my_edges, width), bf16),
        ((my_nodes, width), bf16),
        ((node_count, width), bf16),
        ((node_count, width), bf16),
        ((node_count, width), bf16),
        ((my_nodes, width), bf16),
        ((node_count, share), bf16),
        ((edge_count, width), bf16),
        ((8, width), f32),
        ((mp, 8, share), f32),
        ((8, share), f32),
        ((dom, 8, share), f32),
        ((width, width), bf16),
        ((mp, width, share), bf16),
        ((width, share), bf16),
        ((dom, width // dom, share), bf16),
        ((3 * width, share), bf16),
        ((dom, 3 * width // dom, share), bf16),
        ((width, share), bf16),
        ((dom, width // dom, share), bf16),
        ((2 * width, share), bf16),
        ((dom, 2 * width // dom, share), bf16),
        ((slots, share), bf16),
        ((slots, share), bf16),
        ((edge_count, 2 * share), bf16),
        ((node_count, share), f32),
    ]
    vmem = pl.BlockSpec(memory_space=pltpu.VMEM)
    results = pl.pallas_call(
        functools.partial(fused_kernel, dom, mp, edge_count // node_count),
        out_shape=outs,
        in_specs=[vmem] * 13,
        out_specs=tuple([vmem] * 8),
        scratch_shapes=[pltpu.VMEM(dims, kind) for dims, kind in scratch]
        + [
            pltpu.SemaphoreType.DMA((16, mp - 1)),
            pltpu.SemaphoreType.DMA((16, mp - 1)),
            pltpu.SemaphoreType.DMA((7, dom - 1)),
            pltpu.SemaphoreType.DMA((7, dom - 1)),
            pltpu.SemaphoreType.DMA((21,)),
            pltpu.SemaphoreType.DMA((21,)),
        ],
        compiler_params=pltpu.CompilerParams(
            collective_id=0, has_side_effects=True, vmem_limit_bytes=56 * 1024 * 1024
        ),
        name="layer_backward",
    )(
        node_latents,
        edge_latents,
        node_cotangent,
        edge_cotangent,
        senders.reshape(1, edge_count),
        receivers.reshape(1, edge_count),
        send_nodes.reshape(send_nodes.shape[1:]),
        edge_in_weight.reshape(3, width, share),
        edge_out_weight,
        edge_gain.reshape(1, share),
        node_in_weight,
        node_out_weight,
        node_gain.reshape(1, share),
    )
    anywhere = pl.BlockSpec(memory_space=pl.ANY)
    results = list(
        pl.pallas_call(
            hand_over_kernel,
            out_shape=outs,
            in_specs=[anywhere] * len(outs),
            out_specs=tuple([anywhere] * len(outs)),
            scratch_shapes=[pltpu.SemaphoreType.DMA((len(outs),))],
            name="hand_over",
        )(*results)
    )
    results[4], results[7] = results[4].reshape(share), results[7].reshape(share)
    return tuple(results)


def solution(mesh):
    in_specs = (
        P(("groups", "dom"), None),
        P(("groups", "dom"), None),
        P(("groups", "dom"), "mp"),
        P(("groups", "dom"), "mp"),
        P("dom"),
        P("dom"),
        P("dom", None, None),
        P(None, "mp"),
        P(None, "mp"),
        P("mp"),
        P(None, "mp"),
        P(None, "mp"),
        P("mp"),
    )
    out_specs = (
        P(("groups", "dom"), "mp"),
        P(("groups", "dom"), "mp"),
        P(("groups", "dom"), "mp"),
        P(("groups", "dom"), "mp"),
        P(("groups", "mp")),
        P(("groups", "dom"), "mp"),
        P(("groups", "dom"), "mp"),
        P(("groups", "mp")),
    )
    return jax.shard_map(fused_body if fits_kernel(mesh) else body, mesh=mesh, in_specs=in_specs, out_specs=out_specs, check_vma=False)
```

```python
import functools

import jax
import jax.numpy as jnp
from jax import lax
from jax.experimental import pallas as pl
from jax.experimental.pallas import tpu as pltpu
from jax.sharding import PartitionSpec as P

norm_eps = 1e-05


def shortened(value):

    def short(part):
        return part.astype(jnp.bfloat16) if part.dtype == jnp.float32 else part

    return jax.tree.map(short, value)


def silu_slope(values):
    sigma = jax.nn.sigmoid(values)
    return sigma * (1.0 + values * (1.0 - sigma))


def dot_first(left, right):
    return lax.dot_general(
        left, right, (((0,), (0,)), ((), ())), preferred_element_type=jnp.float32
    )


def dot_last(left, right):
    return lax.dot_general(
        left, right, (((1,), (1,)), ((), ())), preferred_element_type=jnp.float32
    )


def add_rows_into(index, count, values):
    table = (index[:, None] == jnp.arange(count, dtype=jnp.int32)[None, :]).astype(values.dtype)
    if values.dtype == jnp.float32:
        return lax.dot_general(
            table,
            values,
            (((0,), (0,)), ((), ())),
            precision=lax.Precision.HIGHEST,
            preferred_element_type=jnp.float32,
        )
    return dot_first(table, values)


def join_columns(values):
    return jax.tree.map(
        lambda part, own: part.astype(own.dtype),
        lax.all_gather(shortened(values), "mp", axis=1, tiled=True),
        values,
    )


def row_moments(first_term, second_term):
    return lax.psum((jnp.sum(first_term, axis=1), jnp.sum(second_term, axis=1)), "mp")


def swap_crossing(values):
    return lax.all_to_all(values, "dom", split_axis=0, concat_axis=0, tiled=True)


def reduce_grads(values):
    return (
        lax.psum_scatter(
            values[0].astype(jnp.bfloat16), "dom", scatter_dimension=0, tiled=True
        ).astype(jnp.float32),
        lax.psum_scatter(
            values[1].astype(jnp.bfloat16), "dom", scatter_dimension=0, tiled=True
        ).astype(jnp.float32),
    )


def norm_parts(values, latent_width):
    first_sum, second_sum = row_moments(values, values * values)
    center = (first_sum / latent_width)[:, None]
    spread = (second_sum / latent_width)[:, None] - center * center
    scale_inv = lax.rsqrt(spread + norm_eps)
    return ((values - center) * scale_inv, scale_inv)


def norm_back(upstream, gain_row, hatted, scale_inv, latent_width):
    weighted = upstream * gain_row
    first_sum, second_sum = row_moments(weighted, weighted * hatted)
    return scale_inv * (
        weighted
        - (first_sum / latent_width)[:, None]
        - hatted * (second_sum / latent_width)[:, None]
    )


def body(
    node_latents,
    edge_latents,
    node_cotangent,
    edge_cotangent,
    senders,
    receivers,
    send_nodes,
    edge_in_weight,
    edge_out_weight,
    edge_gain,
    node_in_weight,
    node_out_weight,
    node_gain,
):
    dom_count = lax.axis_size("dom")
    mp_count = lax.axis_size("mp")
    nodes_dev, latent_width = node_latents.shape
    edges_dev = edge_latents.shape[0]
    column_share = latent_width // mp_count
    column_start = lax.axis_index("mp") * column_share
    edge_scale = float(edges_dev * dom_count) ** (-0.5)
    node_scale = float(nodes_dev * dom_count) ** (-0.5)
    send_table = send_nodes[0].reshape(-1)
    halo_rows = swap_crossing(node_latents[send_table])
    extended = jnp.concatenate([node_latents, halo_rows], axis=0)
    edge_input = jnp.concatenate([edge_latents, extended[senders], node_latents[receivers]], axis=1)
    edge_pre = jnp.dot(edge_input, edge_in_weight, preferred_element_type=jnp.float32)
    edge_hidden = join_columns(jax.nn.silu(edge_pre).astype(jnp.bfloat16))
    edge_out = jnp.dot(edge_hidden, edge_out_weight, preferred_element_type=jnp.float32)
    edge_hat, edge_rstd = norm_parts(edge_out, latent_width)
    edge_update = (edge_hat * edge_gain).astype(jnp.bfloat16)
    aggregate = add_rows_into(receivers, nodes_dev, edge_update).astype(jnp.bfloat16)
    node_input = jnp.concatenate([node_latents, join_columns(aggregate)], axis=1)
    node_pre = jnp.dot(node_input, node_in_weight, preferred_element_type=jnp.float32)
    node_hidden = join_columns(jax.nn.silu(node_pre).astype(jnp.bfloat16))
    node_out = jnp.dot(node_hidden, node_out_weight, preferred_element_type=jnp.float32)
    node_hat, node_rstd = norm_parts(node_out, latent_width)
    out_edge_full, out_node_full = join_columns((edge_out_weight, node_out_weight))
    in_edge_full, in_node_full = join_columns((edge_in_weight, node_in_weight))
    node_cot = node_cotangent.astype(jnp.float32)
    edge_cot = edge_cotangent.astype(jnp.float32)
    node_gain_part = jnp.sum(node_cot * node_hat, axis=0) * node_scale
    node_slope = norm_back(node_cot, node_gain, node_hat, node_rstd, latent_width).astype(
        jnp.bfloat16
    )
    node_out_part = dot_first(node_hidden, node_slope) * node_scale
    node_slope_full = join_columns(node_slope)
    node_hidden_rows = lax.dynamic_slice_in_dim(out_node_full, column_start, column_share, 0)
    node_delta = (dot_last(node_slope_full, node_hidden_rows) * silu_slope(node_pre)).astype(
        jnp.bfloat16
    )
    node_in_part = dot_first(node_input, node_delta) * node_scale
    node_in_grad, node_out_grad = reduce_grads((node_in_part, node_out_part))
    node_delta_full = join_columns(node_delta)
    node_feature_rows = lax.dynamic_slice_in_dim(
        in_node_full.reshape(2, latent_width, latent_width), column_start, column_share, 1
    )
    node_back = jnp.einsum(
        "nj,bkj->bnk", node_delta_full, node_feature_rows, preferred_element_type=jnp.float32
    )
    update_grad = edge_cot + node_back[1][receivers]
    edge_gain_part = jnp.sum(update_grad * edge_hat, axis=0) * edge_scale
    edge_slope = norm_back(update_grad, edge_gain, edge_hat, edge_rstd, latent_width).astype(
        jnp.bfloat16
    )
    edge_out_part = dot_first(edge_hidden, edge_slope) * edge_scale
    edge_slope_full = join_columns(edge_slope)
    edge_hidden_rows = lax.dynamic_slice_in_dim(out_edge_full, column_start, column_share, 0)
    edge_delta = (dot_last(edge_slope_full, edge_hidden_rows) * silu_slope(edge_pre)).astype(
        jnp.bfloat16
    )
    edge_in_part = dot_first(edge_input, edge_delta) * edge_scale
    edge_delta_full = join_columns(edge_delta)
    edge_feature_rows = lax.dynamic_slice_in_dim(
        in_edge_full.reshape(3, latent_width, latent_width), column_start, column_share, 1
    )
    edge_back = jnp.einsum(
        "ej,bkj->bek", edge_delta_full, edge_feature_rows, preferred_element_type=jnp.float32
    )
    edge_grad = (edge_cot + edge_back[0]).astype(jnp.bfloat16)
    sender_sums = add_rows_into(senders, nodes_dev + send_table.shape[0], edge_back[1])
    returned_rows = swap_crossing(sender_sums[nodes_dev:].astype(jnp.bfloat16))
    returned = add_rows_into(send_table, nodes_dev, returned_rows)
    receiver_sums = add_rows_into(receivers, nodes_dev, edge_back[2])
    node_grad = (
        node_cot + node_back[0] + receiver_sums + sender_sums[:nodes_dev] + returned
    ).astype(jnp.bfloat16)
    edge_in_grad, edge_out_grad = reduce_grads((edge_in_part, edge_out_part))
    edge_gain_grad, node_gain_grad = lax.psum((edge_gain_part, node_gain_part), "dom")
    return (
        node_grad,
        edge_grad,
        edge_in_grad,
        edge_out_grad,
        edge_gain_grad,
        node_in_grad,
        node_out_grad,
        node_gain_grad,
    )


def dot_plain(left, right):
    return jnp.dot(left, right, preferred_element_type=jnp.float32)


def two_terms(values):
    high = values.astype(jnp.bfloat16)
    low = (values - high.astype(jnp.float32)).astype(jnp.bfloat16)
    return jnp.concatenate([high, low], axis=1)


def join_terms(values):
    half = values.shape[1] // 2
    return values[:, :half] + values[:, half:]


def repeat_rows(values, times):
    rows, columns = values.shape
    return jnp.broadcast_to(values[:, None, :], (rows, times, columns)).reshape(
        rows * times, columns
    )


def sum_rows(values, times):
    rows, columns = values.shape
    return jnp.sum(values.reshape(rows // times, times, columns), axis=1)


def local_norm(values):
    center = jnp.mean(values, axis=1, keepdims=True)
    spread = jnp.mean(values * values, axis=1, keepdims=True) - center * center
    scale_inv = lax.rsqrt(spread + norm_eps)
    return (values - center) * scale_inv, scale_inv


def local_norm_back(upstream, gain_row, hatted, scale_inv):
    weighted = upstream * gain_row
    first_mean = jnp.mean(weighted, axis=1, keepdims=True)
    second_mean = jnp.mean(weighted * hatted, axis=1, keepdims=True)
    return scale_inv * (weighted - first_mean - hatted * second_mean)


def fused_kernel(
    dom,
    mp,
    degree,
    nodes,
    edges,
    node_cot,
    edge_cot,
    senders,
    receivers,
    table,
    w_in,
    w_out,
    e_gain,
    nw_in,
    nw_out,
    n_gain,
    node_grad,
    edge_grad,
    edge_in_grad,
    edge_out_grad,
    edge_gain_grad,
    node_in_grad,
    node_out_grad,
    node_gain_grad,
    halo_send,
    extended,
    w_out_all,
    nw_in_all,
    nw_out_all,
    w_in_rows,
    e_gain_all,
    n_gain_all,
    perm,
    edges_sorted,
    cot_sorted,
    grad_sorted,
    sender_hot,
    pre_cols,
    pre_rows,
    cot_rows,
    ncot_rows,
    agg_all,
    nhid_all,
    ndelta_all,
    nslope_own,
    nslope_cols,
    delta_all,
    gain_part,
    gain_recv,
    gain_sum,
    gain_dom,
    eo_part,
    eo_recv,
    eo_send,
    eo_dom,
    ei_send,
    ei_dom,
    no_send,
    no_dom,
    ni_send,
    ni_dom,
    cross_send,
    cross_recv,
    back_terms,
    receiver_back,
    receiver_pre,
    mp_send_sem,
    mp_recv_sem,
    dom_send_sem,
    dom_recv_sem,
    one_send_sem,
    one_recv_sem,
):
    f32, bf16 = jnp.float32, jnp.bfloat16
    node_count, width = nodes.shape
    edge_count = edges.shape[0]
    share = width // mp
    my_nodes, my_edges = node_count // mp, edge_count // mp
    cap = table.shape[1]
    slots = dom * cap
    edge_scale = float(edge_count * dom) ** (-0.5)
    node_scale = float(node_count * dom) ** (-0.5)
    me_m, me_d = lax.axis_index("mp"), lax.axis_index("dom")

    def rows(index, size):
        return pl.ds(pl.multiple_of(index * size, size), size)

    me_g = lax.axis_index("groups")
    mate = me_m + 1 - 2 * lax.rem(me_m, 2)
    across = lax.rem(me_m + 2, mp)
    across_mate = lax.rem(mate + 2, mp)
    mp_to = [lax.rem(me_m + k, mp) for k in range(1, mp)]
    mp_from = [lax.rem(me_m + mp - k, mp) for k in range(1, mp)]
    dom_to = [lax.rem(me_d + k, dom) for k in range(1, dom)]
    dom_from = [lax.rem(me_d + dom - k, dom) for k in range(1, dom)]
    started = []

    def push(axis, kind, peers, source, target):
        send, recv = (
            (mp_send_sem, mp_recv_sem) if axis == "mp" else (dom_send_sem, dom_recv_sem)
        )
        copies = []
        for k, peer in enumerate(peers):
            copy = pltpu.make_async_remote_copy(
                src_ref=source(peer),
                dst_ref=target,
                send_sem=send.at[kind, k],
                recv_sem=recv.at[kind, k],
                device_id={axis: peer},
                device_id_type=pl.DeviceIdType.MESH,
            )
            copy.start()
            copies.append(copy)
        started.extend(copies)
        return copies

    used = iter(range(one_send_sem.shape[0]))

    def put(device, source, target):
        slot = next(used)
        copy = pltpu.make_async_remote_copy(
            src_ref=source,
            dst_ref=target,
            send_sem=one_send_sem.at[slot],
            recv_sem=one_recv_sem.at[slot],
            device_id=device,
            device_id_type=pl.DeviceIdType.MESH,
        )
        copy.start()
        started.append(copy)
        return copy

    def arrived(copies):
        for copy in copies:
            copy.wait_recv()

    barrier = pltpu.get_barrier_semaphore()
    for axis, peers in (("mp", mp_to), ("dom", dom_to), ("groups", [1 - me_g])):
        for peer in peers:
            pl.semaphore_signal(
                barrier, inc=1, device_id={axis: peer}, device_id_type=pl.DeviceIdType.MESH
            )

    table_row = jnp.concatenate([table[p : p + 1, :] for p in range(dom)], axis=1)
    table_hot = (
        lax.broadcasted_iota(jnp.int32, (node_count, slots), 0) == table_row
    ).astype(bf16)
    halo_send[...] = dot_first(table_hot, nodes[...]).astype(bf16)
    extended[pl.ds(0, node_count), :] = nodes[...]
    extended[pl.ds(pl.multiple_of(node_count + me_d * cap, cap), cap), :] = jnp.zeros(
        (cap, width), bf16
    )
    pl.semaphore_wait(barrier, mp + dom - 1)

    halo = push(
        "dom",
        0,
        dom_to,
        lambda peer: halo_send.at[rows(peer, cap), :],
        extended.at[pl.ds(pl.multiple_of(node_count + me_d * cap, cap), cap), :],
    )
    own_cols = rows(me_m, share)
    across_cols = rows(across, share)

    def weight_first(weight, whole):
        half = rows(me_g, weight.shape[0] // 2)
        return [
            put({"mp": across}, weight.at[half, :], whole.at[half, own_cols]),
            put({"mp": mate}, weight, whole.at[:, own_cols]),
        ]

    def weight_second(first, whole):
        first[0].wait_recv()
        part = whole.at[rows(me_g, whole.shape[0] // 2), across_cols]
        return first[1:] + [
            put({"groups": 1 - me_g}, part, part),
            put({"mp": mate}, part, part),
        ]

    def weight_third(second, whole):
        second[1].wait_recv()
        part = whole.at[rows(1 - me_g, whole.shape[0] // 2), across_cols]
        return [second[0], second[2], put({"mp": mate}, part, part)]

    w_out_in = weight_first(w_out, w_out_all)
    nw_in_in = weight_first(nw_in, nw_in_all)
    nw_out_in = weight_first(nw_out, nw_out_all)
    gain_in = push("mp", 1, mp_to, lambda peer: e_gain, e_gain_all.at[:, own_cols])
    ngain_in = push("mp", 2, mp_to, lambda peer: n_gain, n_gain_all.at[:, own_cols])
    ncot_in = push(
        "mp", 3, mp_to, lambda peer: node_cot.at[rows(peer, my_nodes), :], ncot_rows.at[:, own_cols]
    )
    w_out_all[:, own_cols] = w_out[...]
    e_gain_all[:, own_cols] = e_gain[...]
    n_gain_all[:, own_cols] = n_gain[...]
    ncot_rows[:, own_cols] = node_cot[rows(me_m, my_nodes), :]
    nw_in_all[:, own_cols] = nw_in[...]
    nw_out_all[:, own_cols] = nw_out[...]
    w_in_rows[:, :, own_cols] = w_in[:, rows(me_m, share), :]

    lane = 128
    before = (
        lax.broadcasted_iota(jnp.int32, (lane, lane), 0)
        < lax.broadcasted_iota(jnp.int32, (lane, lane), 1)
    ).astype(bf16)
    offset = jnp.zeros((node_count, 1), f32)
    places = []
    for start in range(0, edge_count, lane):
        received = receivers[:, start : start + lane]
        hot = lax.broadcasted_iota(jnp.int32, (node_count, lane), 0) == received
        hot32 = hot.astype(f32)
        earlier = dot_plain(hot32.astype(bf16), before) + offset
        rank = jnp.sum(hot32 * earlier, axis=0, keepdims=True)
        places.append(received * degree + rank.astype(jnp.int32))
        offset = offset + jnp.sum(hot32, axis=1, keepdims=True)
    place = jnp.concatenate(places, axis=1)
    sender_cols = (
        lax.broadcasted_iota(jnp.int32, (node_count + slots, edge_count), 0) == senders[...]
    ).astype(bf16)
    receiver_pre[...] = dot_plain(nodes[...], w_in[2])
    owners = [across, across_mate, mate, me_m]
    cot_in = []
    for step, owner in enumerate(owners):
        block = rows(owner, my_edges)
        hot = (
            lax.broadcasted_iota(jnp.int32, (my_edges, edge_count), 0) + owner * my_edges == place
        ).astype(bf16)
        perm[block, :] = hot
        cot_sorted[block, :] = dot_plain(hot, edge_cot[...]).astype(bf16)
        if step < mp - 1:
            cot_in.append(put({"mp": owner}, cot_sorted.at[block, :], cot_rows.at[:, own_cols]))
        edges_sorted[block, :] = dot_plain(hot, edges[...]).astype(bf16)
        sender_hot[block, :] = dot_last(hot, sender_cols).astype(bf16)
        if step == mp // 2:
            w_out_in = weight_second(w_out_in, w_out_all)
    nw_in_in = weight_second(nw_in_in, nw_in_all)
    nw_out_in = weight_second(nw_out_in, nw_out_all)
    arrived(halo)
    sender_pre = two_terms(dot_plain(extended[...], w_in[1]))
    pre_in = []
    for step, owner in enumerate(owners):
        block = rows(owner, my_edges)
        local = dot_plain(edges_sorted[block, :], w_in[0])
        local = local + repeat_rows(receiver_pre[rows(owner, my_nodes), :], degree)
        local = local + join_terms(dot_plain(sender_hot[block, :], sender_pre))
        pre_cols[block, :] = local.astype(bf16)
        if step < mp - 1:
            pre_in.append(put({"mp": owner}, pre_cols.at[block, :], pre_rows.at[:, own_cols]))
    pre_rows[:, own_cols] = pre_cols[rows(me_m, my_edges), :]
    cot_rows[:, own_cols] = cot_sorted[rows(me_m, my_edges), :]

    w_out_in = weight_third(w_out_in, w_out_all)
    arrived(pre_in)
    w_in_in = push(
        "mp", 8, mp_to, lambda peer: w_in.at[:, rows(peer, share), :], w_in_rows.at[:, :, own_cols]
    )
    edge_pre = pre_rows[...].astype(f32)
    edge_hidden = (edge_pre * jax.nn.sigmoid(edge_pre)).astype(bf16)
    arrived(w_out_in)
    edge_out = dot_plain(edge_hidden, w_out_all[...])
    edge_hat, edge_rstd = local_norm(edge_out)
    arrived(gain_in)
    edge_update = (edge_hat * e_gain_all[...]).astype(bf16).astype(f32)
    own_rows = rows(me_m, my_nodes)
    aggregate = sum_rows(edge_update, degree).astype(bf16)
    agg_all[own_rows, :] = aggregate
    agg_in = push(
        "mp", 9, mp_to, lambda peer: agg_all.at[own_rows, :], agg_all.at[own_rows, :]
    )
    nw_in_in = weight_third(nw_in_in, nw_in_all)
    nw_out_in = weight_third(nw_out_in, nw_out_all)
    arrived(nw_in_in)
    node_pre = dot_plain(nodes[own_rows, :], nw_in_all[pl.ds(0, width), :]) + dot_plain(
        aggregate, nw_in_all[pl.ds(width, width), :]
    )
    node_hidden = (node_pre * jax.nn.sigmoid(node_pre)).astype(bf16)
    nhid_all[own_rows, :] = node_hidden
    nhid_in = push(
        "mp", 10, mp_to, lambda peer: nhid_all.at[own_rows, :], nhid_all.at[own_rows, :]
    )
    arrived(nw_out_in)
    node_hat, node_rstd = local_norm(dot_plain(node_hidden, nw_out_all[...]))
    arrived(ncot_in)
    arrived(ngain_in)
    ncot = ncot_rows[...].astype(f32)
    gain_part[...] = jnp.zeros_like(gain_part)
    gain_part[0:1, :] = jnp.sum(ncot * node_hat, axis=0, keepdims=True) * node_scale
    node_slope = local_norm_back(ncot, n_gain_all[...], node_hat, node_rstd).astype(bf16)
    nslope_own[...] = node_slope
    nslope_in = push(
        "mp", 11, mp_to, lambda peer: nslope_own.at[:, rows(peer, share)], nslope_cols.at[own_rows, :]
    )
    nslope_cols[own_rows, :] = nslope_own[:, own_cols]
    node_delta = (dot_last(node_slope, nw_out_all[...]) * silu_slope(node_pre)).astype(bf16)
    ndelta_all[own_rows, :] = node_delta
    ndelta_in = push(
        "mp", 12, mp_to, lambda peer: ndelta_all.at[own_rows, :], ndelta_all.at[own_rows, :]
    )
    agg_back = dot_last(node_delta, nw_in_all[pl.ds(width, width), :])
    arrived(cot_in)
    update_grad = cot_rows[...].astype(f32) + repeat_rows(agg_back, degree)
    gain_part[1:2, :] = jnp.sum(update_grad * edge_hat, axis=0, keepdims=True) * edge_scale
    edge_slope = local_norm_back(update_grad, e_gain_all[...], edge_hat, edge_rstd).astype(bf16)
    edge_pre = pre_rows[...].astype(f32)
    edge_delta = (dot_last(edge_slope, w_out_all[...]) * silu_slope(edge_pre)).astype(bf16)
    own_edges = rows(me_m, my_edges)
    delta_all[own_edges, :] = edge_delta
    cols = [rows(owner, share) for owner in owners]

    def delta_piece(device, owner, col):
        piece = delta_all.at[rows(owner, my_edges), col]
        return put({"mp": device}, piece, piece)

    delta_own_cols = [delta_piece(across, me_m, cols[0]), delta_piece(across_mate, me_m, cols[1])]
    own_delta = delta_all.at[own_edges, :]
    delta_mate = put({"mp": mate}, own_delta, own_delta)
    gain_part_in = push(
        "mp", 15, mp_to, lambda peer: gain_part.at[:, rows(peer, share)], gain_recv.at[me_m]
    )
    gain_recv[me_m] = gain_part[:, own_cols]

    arrived(agg_in)
    arrived(nhid_in)
    arrived(nslope_in)
    arrived(ndelta_in)
    no_send[...] = (dot_first(nhid_all[...], nslope_cols[...]) * node_scale).astype(bf16)
    ndelta_cols = ndelta_all[:, own_cols]
    ni_send[pl.ds(0, width), :] = (dot_first(nodes[...], ndelta_cols) * node_scale).astype(bf16)
    ni_send[pl.ds(width, width), :] = (dot_first(agg_all[...], ndelta_cols) * node_scale).astype(
        bf16
    )

    def scatter_sum(kind, parts, landed):
        size = landed.shape[1]
        copies = push(
            "dom", kind, dom_to, lambda peer: parts.at[rows(peer, size), :], landed.at[me_d]
        )
        landed[me_d] = parts[rows(me_d, size), :]
        return copies

    no_in = scatter_sum(1, no_send, no_dom)
    ni_in = scatter_sum(2, ni_send, ni_dom)
    total = node_cot[...].astype(f32) + dot_last(ndelta_all[...], nw_in_all[own_cols, :])

    eo_part[...] = (dot_first(edge_hidden, edge_slope) * edge_scale).astype(bf16)
    eo_in = [
        put({"mp": mate}, eo_part.at[:, rows(mate, share)], eo_recv.at[0]),
        put({"mp": mate}, eo_part.at[:, rows(across_mate, share)], eo_recv.at[1]),
    ]
    delta_rest = [delta_piece(across, me_m, col) for col in cols[1:]]
    delta_mate.wait_recv()
    arrived(delta_own_cols)
    delta_cols = delta_all[:, own_cols]
    own_scale = jnp.float32(edge_scale)
    ei_send[pl.ds(0, width), :] = (dot_first(edges_sorted[...], delta_cols) * own_scale).astype(
        bf16
    )
    by_sender = two_terms(dot_first(sender_hot[...], delta_cols))
    ei_send[pl.ds(width, width), :] = (
        join_terms(dot_first(extended[...], by_sender)) * own_scale
    ).astype(bf16)
    by_receiver = two_terms(sum_rows(delta_cols.astype(f32), degree))
    ei_send[pl.ds(2 * width, width), :] = (
        join_terms(dot_first(nodes[...], by_receiver)) * own_scale
    ).astype(bf16)
    ei_in = scatter_sum(4, ei_send, ei_dom)
    arrived(eo_in)
    eo_recv[2] = (eo_part[:, across_cols].astype(f32) + eo_recv[1].astype(f32)).astype(bf16)
    eo_across = put({"mp": across}, eo_recv.at[2], eo_recv.at[3])

    arrived(w_in_in)

    def input_back(owner):
        block = rows(owner, my_edges)
        deltas = delta_all[block, :]
        grad = cot_sorted[block, :].astype(f32) + dot_last(deltas, w_in_rows[0])
        grad_sorted[block, :] = grad.astype(bf16)
        back_terms[block, :] = two_terms(dot_last(deltas, w_in_rows[1]))
        receiver_back[rows(owner, my_nodes), :] = sum_rows(
            dot_last(deltas, w_in_rows[2]), degree
        )

    input_back(me_m)
    input_back(mate)
    arrived(delta_rest)
    delta_last = [delta_piece(mate, across, col) for col in (cols[3], cols[0], cols[1])]
    eo_across.wait_recv()
    eo_send[...] = (
        eo_part[:, own_cols].astype(f32) + eo_recv[0].astype(f32) + eo_recv[3].astype(f32)
    ).astype(bf16)
    eo_out = scatter_sum(5, eo_send, eo_dom)
    input_back(across)
    arrived(delta_last)
    input_back(across_mate)
    sender_sums = join_terms(dot_first(sender_hot[...], back_terms[...]))
    cross_send[...] = sender_sums[node_count:].astype(bf16)
    cross_recv[rows(me_d, cap), :] = jnp.zeros((cap, share), bf16)
    cross_in = push(
        "dom",
        3,
        dom_to,
        lambda peer: cross_send.at[rows(peer, cap), :],
        cross_recv.at[rows(me_d, cap), :],
    )
    arrived(gain_part_in)
    gain_sum[...] = jnp.sum(gain_recv[...], axis=0)
    gain_out = push("dom", 6, dom_to, lambda peer: gain_sum, gain_dom.at[me_d])
    gain_dom[me_d] = gain_sum[...]

    edge_grad[...] = dot_first(perm[...], grad_sorted[...]).astype(bf16)
    arrived(no_in)
    node_out_grad[...] = jnp.sum(no_dom[...].astype(f32), axis=0)
    arrived(ni_in)
    node_in_grad[...] = jnp.sum(ni_dom[...].astype(f32), axis=0)
    arrived(cross_in)
    node_grad[...] = (
        total + receiver_back[...] + sender_sums[:node_count] + dot_plain(table_hot, cross_recv[...])
    ).astype(bf16)
    arrived(gain_out)
    gains = jnp.sum(gain_dom[...], axis=0)
    node_gain_grad[...] = gains[0:1]
    edge_gain_grad[...] = gains[1:2]
    arrived(eo_out)
    edge_out_grad[...] = jnp.sum(eo_dom[...].astype(f32), axis=0)
    arrived(ei_in)
    edge_in_grad[...] = jnp.sum(ei_dom[...].astype(f32), axis=0)
    for copy in started:
        copy.wait_send()


def fits_kernel(mesh):
    return mesh.shape["groups"] == 2 and mesh.shape["mp"] == 4 and mesh.shape["dom"] <= 8


def hand_over_kernel(*refs):
    count = len(refs) // 2
    for source, target in zip(refs[:count], refs[count:]):
        target[...] = source[...]


def fused_body(
    node_latents,
    edge_latents,
    node_cotangent,
    edge_cotangent,
    senders,
    receivers,
    send_nodes,
    edge_in_weight,
    edge_out_weight,
    edge_gain,
    node_in_weight,
    node_out_weight,
    node_gain,
):
    dom, mp = lax.axis_size("dom"), lax.axis_size("mp")
    node_count, width = node_latents.shape
    edge_count = edge_latents.shape[0]
    slots = send_nodes.shape[1] * send_nodes.shape[2]
    share = width // mp
    my_nodes, my_edges = node_count // mp, edge_count // mp
    f32, bf16 = jnp.float32, jnp.bfloat16
    shape = jax.ShapeDtypeStruct
    outs = (
        shape((node_count, share), bf16),
        shape((edge_count, share), bf16),
        shape((3 * width // dom, share), f32),
        shape((width // dom, share), f32),
        shape((1, share), f32),
        shape((2 * width // dom, share), f32),
        shape((width // dom, share), f32),
        shape((1, share), f32),
    )
    scratch = [
        ((slots, width), bf16),
        ((node_count + slots, width), bf16),
        ((width, width), bf16),
        ((2 * width, width), bf16),
        ((width, width), bf16),
        ((3, share, width), bf16),
        ((1, width), f32),
        ((1, width), f32),
        ((edge_count, edge_count), bf16),
        ((edge_count, width), bf16),
        ((edge_count, share), bf16),
        ((edge_count, share), bf16),
        ((edge_count, node_count + slots), bf16),
        ((edge_count, share), bf16),
        ((my_edges, width), bf16),
        ((my_edges, width), bf16),
        ((my_nodes, width), bf16),
        ((node_count, width), bf16),
        ((node_count, width), bf16),
        ((node_count, width), bf16),
        ((my_nodes, width), bf16),
        ((node_count, share), bf16),
        ((edge_count, width), bf16),
        ((8, width), f32),
        ((mp, 8, share), f32),
        ((8, share), f32),
        ((dom, 8, share), f32),
        ((width, width), bf16),
        ((mp, width, share), bf16),
        ((width, share), bf16),
        ((dom, width // dom, share), bf16),
        ((3 * width, share), bf16),
        ((dom, 3 * width // dom, share), bf16),
        ((width, share), bf16),
        ((dom, width // dom, share), bf16),
        ((2 * width, share), bf16),
        ((dom, 2 * width // dom, share), bf16),
        ((slots, share), bf16),
        ((slots, share), bf16),
        ((edge_count, 2 * share), bf16),
        ((node_count, share), f32),
        ((node_count, share), f32),
    ]
    vmem = pl.BlockSpec(memory_space=pltpu.VMEM)
    results = pl.pallas_call(
        functools.partial(fused_kernel, dom, mp, edge_count // node_count),
        out_shape=outs,
        in_specs=[vmem] * 13,
        out_specs=tuple([vmem] * 8),
        scratch_shapes=[pltpu.VMEM(dims, kind) for dims, kind in scratch]
        + [
            pltpu.SemaphoreType.DMA((16, mp - 1)),
            pltpu.SemaphoreType.DMA((16, mp - 1)),
            pltpu.SemaphoreType.DMA((7, dom - 1)),
            pltpu.SemaphoreType.DMA((7, dom - 1)),
            pltpu.SemaphoreType.DMA((40,)),
            pltpu.SemaphoreType.DMA((40,)),
        ],
        compiler_params=pltpu.CompilerParams(
            collective_id=0, has_side_effects=True, vmem_limit_bytes=56 * 1024 * 1024
        ),
        name="layer_backward",
    )(
        node_latents,
        edge_latents,
        node_cotangent,
        edge_cotangent,
        senders.reshape(1, edge_count),
        receivers.reshape(1, edge_count),
        send_nodes.reshape(send_nodes.shape[1:]),
        edge_in_weight.reshape(3, width, share),
        edge_out_weight,
        edge_gain.reshape(1, share),
        node_in_weight,
        node_out_weight,
        node_gain.reshape(1, share),
    )
    results = list(
        pl.pallas_call(
            hand_over_kernel,
            out_shape=outs,
            in_specs=[vmem] * len(outs),
            out_specs=tuple([vmem] * len(outs)),
            name="hand_over",
        )(*results)
    )
    results[4], results[7] = results[4].reshape(share), results[7].reshape(share)
    return tuple(results)


def solution(mesh):
    in_specs = (
        P(("groups", "dom"), None),
        P(("groups", "dom"), None),
        P(("groups", "dom"), "mp"),
        P(("groups", "dom"), "mp"),
        P("dom"),
        P("dom"),
        P("dom", None, None),
        P(None, "mp"),
        P(None, "mp"),
        P("mp"),
        P(None, "mp"),
        P(None, "mp"),
        P("mp"),
    )
    out_specs = (
        P(("groups", "dom"), "mp"),
        P(("groups", "dom"), "mp"),
        P(("groups", "dom"), "mp"),
        P(("groups", "dom"), "mp"),
        P(("groups", "mp")),
        P(("groups", "dom"), "mp"),
        P(("groups", "dom"), "mp"),
        P(("groups", "mp")),
    )
    return jax.shard_map(fused_body if fits_kernel(mesh) else body, mesh=mesh, in_specs=in_specs, out_specs=out_specs, check_vma=False)
```

```python
import functools

import jax
import jax.numpy as jnp
from jax import lax
from jax.experimental import pallas as pl
from jax.experimental.pallas import tpu as pltpu
from jax.sharding import PartitionSpec as P

norm_eps = 1e-05


def shortened(value):

    def short(part):
        return part.astype(jnp.bfloat16) if part.dtype == jnp.float32 else part

    return jax.tree.map(short, value)


def silu_slope(values):
    sigma = jax.nn.sigmoid(values)
    return sigma * (1.0 + values * (1.0 - sigma))


def dot_first(left, right):
    return lax.dot_general(
        left, right, (((0,), (0,)), ((), ())), preferred_element_type=jnp.float32
    )


def dot_last(left, right):
    return lax.dot_general(
        left, right, (((1,), (1,)), ((), ())), preferred_element_type=jnp.float32
    )


def add_rows_into(index, count, values):
    table = (index[:, None] == jnp.arange(count, dtype=jnp.int32)[None, :]).astype(values.dtype)
    if values.dtype == jnp.float32:
        return lax.dot_general(
            table,
            values,
            (((0,), (0,)), ((), ())),
            precision=lax.Precision.HIGHEST,
            preferred_element_type=jnp.float32,
        )
    return dot_first(table, values)


def join_columns(values):
    return jax.tree.map(
        lambda part, own: part.astype(own.dtype),
        lax.all_gather(shortened(values), "mp", axis=1, tiled=True),
        values,
    )


def row_moments(first_term, second_term):
    return lax.psum((jnp.sum(first_term, axis=1), jnp.sum(second_term, axis=1)), "mp")


def swap_crossing(values):
    return lax.all_to_all(values, "dom", split_axis=0, concat_axis=0, tiled=True)


def reduce_grads(values):
    return (
        lax.psum_scatter(
            values[0].astype(jnp.bfloat16), "dom", scatter_dimension=0, tiled=True
        ).astype(jnp.float32),
        lax.psum_scatter(
            values[1].astype(jnp.bfloat16), "dom", scatter_dimension=0, tiled=True
        ).astype(jnp.float32),
    )


def norm_parts(values, latent_width):
    first_sum, second_sum = row_moments(values, values * values)
    center = (first_sum / latent_width)[:, None]
    spread = (second_sum / latent_width)[:, None] - center * center
    scale_inv = lax.rsqrt(spread + norm_eps)
    return ((values - center) * scale_inv, scale_inv)


def norm_back(upstream, gain_row, hatted, scale_inv, latent_width):
    weighted = upstream * gain_row
    first_sum, second_sum = row_moments(weighted, weighted * hatted)
    return scale_inv * (
        weighted
        - (first_sum / latent_width)[:, None]
        - hatted * (second_sum / latent_width)[:, None]
    )


def body(
    node_latents,
    edge_latents,
    node_cotangent,
    edge_cotangent,
    senders,
    receivers,
    send_nodes,
    edge_in_weight,
    edge_out_weight,
    edge_gain,
    node_in_weight,
    node_out_weight,
    node_gain,
):
    dom_count = lax.axis_size("dom")
    mp_count = lax.axis_size("mp")
    nodes_dev, latent_width = node_latents.shape
    edges_dev = edge_latents.shape[0]
    column_share = latent_width // mp_count
    column_start = lax.axis_index("mp") * column_share
    edge_scale = float(edges_dev * dom_count) ** (-0.5)
    node_scale = float(nodes_dev * dom_count) ** (-0.5)
    send_table = send_nodes[0].reshape(-1)
    halo_rows = swap_crossing(node_latents[send_table])
    extended = jnp.concatenate([node_latents, halo_rows], axis=0)
    edge_input = jnp.concatenate([edge_latents, extended[senders], node_latents[receivers]], axis=1)
    edge_pre = jnp.dot(edge_input, edge_in_weight, preferred_element_type=jnp.float32)
    edge_hidden = join_columns(jax.nn.silu(edge_pre).astype(jnp.bfloat16))
    edge_out = jnp.dot(edge_hidden, edge_out_weight, preferred_element_type=jnp.float32)
    edge_hat, edge_rstd = norm_parts(edge_out, latent_width)
    edge_update = (edge_hat * edge_gain).astype(jnp.bfloat16)
    aggregate = add_rows_into(receivers, nodes_dev, edge_update).astype(jnp.bfloat16)
    node_input = jnp.concatenate([node_latents, join_columns(aggregate)], axis=1)
    node_pre = jnp.dot(node_input, node_in_weight, preferred_element_type=jnp.float32)
    node_hidden = join_columns(jax.nn.silu(node_pre).astype(jnp.bfloat16))
    node_out = jnp.dot(node_hidden, node_out_weight, preferred_element_type=jnp.float32)
    node_hat, node_rstd = norm_parts(node_out, latent_width)
    out_edge_full, out_node_full = join_columns((edge_out_weight, node_out_weight))
    in_edge_full, in_node_full = join_columns((edge_in_weight, node_in_weight))
    node_cot = node_cotangent.astype(jnp.float32)
    edge_cot = edge_cotangent.astype(jnp.float32)
    node_gain_part = jnp.sum(node_cot * node_hat, axis=0) * node_scale
    node_slope = norm_back(node_cot, node_gain, node_hat, node_rstd, latent_width).astype(
        jnp.bfloat16
    )
    node_out_part = dot_first(node_hidden, node_slope) * node_scale
    node_slope_full = join_columns(node_slope)
    node_hidden_rows = lax.dynamic_slice_in_dim(out_node_full, column_start, column_share, 0)
    node_delta = (dot_last(node_slope_full, node_hidden_rows) * silu_slope(node_pre)).astype(
        jnp.bfloat16
    )
    node_in_part = dot_first(node_input, node_delta) * node_scale
    node_in_grad, node_out_grad = reduce_grads((node_in_part, node_out_part))
    node_delta_full = join_columns(node_delta)
    node_feature_rows = lax.dynamic_slice_in_dim(
        in_node_full.reshape(2, latent_width, latent_width), column_start, column_share, 1
    )
    node_back = jnp.einsum(
        "nj,bkj->bnk", node_delta_full, node_feature_rows, preferred_element_type=jnp.float32
    )
    update_grad = edge_cot + node_back[1][receivers]
    edge_gain_part = jnp.sum(update_grad * edge_hat, axis=0) * edge_scale
    edge_slope = norm_back(update_grad, edge_gain, edge_hat, edge_rstd, latent_width).astype(
        jnp.bfloat16
    )
    edge_out_part = dot_first(edge_hidden, edge_slope) * edge_scale
    edge_slope_full = join_columns(edge_slope)
    edge_hidden_rows = lax.dynamic_slice_in_dim(out_edge_full, column_start, column_share, 0)
    edge_delta = (dot_last(edge_slope_full, edge_hidden_rows) * silu_slope(edge_pre)).astype(
        jnp.bfloat16
    )
    edge_in_part = dot_first(edge_input, edge_delta) * edge_scale
    edge_delta_full = join_columns(edge_delta)
    edge_feature_rows = lax.dynamic_slice_in_dim(
        in_edge_full.reshape(3, latent_width, latent_width), column_start, column_share, 1
    )
    edge_back = jnp.einsum(
        "ej,bkj->bek", edge_delta_full, edge_feature_rows, preferred_element_type=jnp.float32
    )
    edge_grad = (edge_cot + edge_back[0]).astype(jnp.bfloat16)
    sender_sums = add_rows_into(senders, nodes_dev + send_table.shape[0], edge_back[1])
    returned_rows = swap_crossing(sender_sums[nodes_dev:].astype(jnp.bfloat16))
    returned = add_rows_into(send_table, nodes_dev, returned_rows)
    receiver_sums = add_rows_into(receivers, nodes_dev, edge_back[2])
    node_grad = (
        node_cot + node_back[0] + receiver_sums + sender_sums[:nodes_dev] + returned
    ).astype(jnp.bfloat16)
    edge_in_grad, edge_out_grad = reduce_grads((edge_in_part, edge_out_part))
    edge_gain_grad, node_gain_grad = lax.psum((edge_gain_part, node_gain_part), "dom")
    return (
        node_grad,
        edge_grad,
        edge_in_grad,
        edge_out_grad,
        edge_gain_grad,
        node_in_grad,
        node_out_grad,
        node_gain_grad,
    )


def dot_plain(left, right):
    return jnp.dot(left, right, preferred_element_type=jnp.float32)


def two_terms(values):
    high = values.astype(jnp.bfloat16)
    low = (values - high.astype(jnp.float32)).astype(jnp.bfloat16)
    return jnp.concatenate([high, low], axis=1)


def join_terms(values):
    half = values.shape[1] // 2
    return values[:, :half] + values[:, half:]


def repeat_rows(values, times):
    rows, columns = values.shape
    return jnp.broadcast_to(values[:, None, :], (rows, times, columns)).reshape(
        rows * times, columns
    )


def sum_rows(values, times):
    rows, columns = values.shape
    return jnp.sum(values.reshape(rows // times, times, columns), axis=1)


def local_norm(values):
    center = jnp.mean(values, axis=1, keepdims=True)
    spread = jnp.mean(values * values, axis=1, keepdims=True) - center * center
    scale_inv = lax.rsqrt(spread + norm_eps)
    return (values - center) * scale_inv, scale_inv


def local_norm_back(upstream, gain_row, hatted, scale_inv):
    weighted = upstream * gain_row
    first_mean = jnp.mean(weighted, axis=1, keepdims=True)
    second_mean = jnp.mean(weighted * hatted, axis=1, keepdims=True)
    return scale_inv * (weighted - first_mean - hatted * second_mean)


def fused_kernel(
    dom,
    mp,
    degree,
    nodes,
    edges,
    node_cot,
    edge_cot,
    senders,
    receivers,
    table,
    w_in,
    w_out,
    e_gain,
    nw_in,
    nw_out,
    n_gain,
    node_grad,
    edge_grad,
    edge_in_grad,
    edge_out_grad,
    edge_gain_grad,
    node_in_grad,
    node_out_grad,
    node_gain_grad,
    halo_send,
    extended,
    w_out_all,
    nw_in_all,
    nw_out_all,
    w_in_rows,
    e_gain_all,
    n_gain_all,
    perm,
    edges_sorted,
    cot_sorted,
    grad_sorted,
    sender_hot,
    pre_cols,
    pre_rows,
    cot_rows,
    ncot_rows,
    agg_all,
    nhid_all,
    ndelta_all,
    nslope_own,
    nslope_cols,
    delta_all,
    gain_part,
    gain_recv,
    gain_sum,
    gain_dom,
    eo_part,
    eo_recv,
    eo_send,
    eo_dom,
    ei_send,
    ei_dom,
    no_send,
    no_dom,
    ni_send,
    ni_dom,
    cross_send,
    cross_recv,
    back_terms,
    receiver_back,
    receiver_pre,
    mp_send_sem,
    mp_recv_sem,
    dom_send_sem,
    dom_recv_sem,
    one_send_sem,
    one_recv_sem,
):
    f32, bf16 = jnp.float32, jnp.bfloat16
    node_count, width = nodes.shape
    edge_count = edges.shape[0]
    share = width // mp
    my_nodes, my_edges = node_count // mp, edge_count // mp
    cap = table.shape[1]
    slots = dom * cap
    edge_scale = float(edge_count * dom) ** (-0.5)
    node_scale = float(node_count * dom) ** (-0.5)
    me_m, me_d = lax.axis_index("mp"), lax.axis_index("dom")

    def rows(index, size):
        return pl.ds(pl.multiple_of(index * size, size), size)

    me_g = lax.axis_index("groups")
    mate = me_m + 1 - 2 * lax.rem(me_m, 2)
    across = lax.rem(me_m + 2, mp)
    across_mate = lax.rem(mate + 2, mp)
    mp_to = [lax.rem(me_m + k, mp) for k in range(1, mp)]
    mp_from = [lax.rem(me_m + mp - k, mp) for k in range(1, mp)]
    dom_to = [lax.rem(me_d + k, dom) for k in range(1, dom)]
    dom_from = [lax.rem(me_d + dom - k, dom) for k in range(1, dom)]
    started = []

    def push(axis, kind, peers, source, target):
        send, recv = (
            (mp_send_sem, mp_recv_sem) if axis == "mp" else (dom_send_sem, dom_recv_sem)
        )
        copies = []
        for k, peer in enumerate(peers):
            copy = pltpu.make_async_remote_copy(
                src_ref=source(peer),
                dst_ref=target,
                send_sem=send.at[kind, k],
                recv_sem=recv.at[kind, k],
                device_id={axis: peer},
                device_id_type=pl.DeviceIdType.MESH,
            )
            copy.start()
            copies.append(copy)
        started.extend(copies)
        return copies

    used = iter(range(one_send_sem.shape[0]))

    def put(device, source, target):
        slot = next(used)
        copy = pltpu.make_async_remote_copy(
            src_ref=source,
            dst_ref=target,
            send_sem=one_send_sem.at[slot],
            recv_sem=one_recv_sem.at[slot],
            device_id=device,
            device_id_type=pl.DeviceIdType.MESH,
        )
        copy.start()
        started.append(copy)
        return copy

    def arrived(copies):
        for copy in copies:
            copy.wait_recv()

    barrier = pltpu.get_barrier_semaphore()
    for axis, peers in (("mp", mp_to), ("dom", dom_to), ("groups", [1 - me_g])):
        for peer in peers:
            pl.semaphore_signal(
                barrier, inc=1, device_id={axis: peer}, device_id_type=pl.DeviceIdType.MESH
            )

    table_row = jnp.concatenate([table[p : p + 1, :] for p in range(dom)], axis=1)
    table_hot = (
        lax.broadcasted_iota(jnp.int32, (node_count, slots), 0) == table_row
    ).astype(bf16)
    halo_send[...] = dot_first(table_hot, nodes[...]).astype(bf16)
    extended[pl.ds(0, node_count), :] = nodes[...]
    extended[pl.ds(pl.multiple_of(node_count + me_d * cap, cap), cap), :] = jnp.zeros(
        (cap, width), bf16
    )
    pl.semaphore_wait(barrier, mp + dom - 1)

    halo = push(
        "dom",
        0,
        dom_to,
        lambda peer: halo_send.at[rows(peer, cap), :],
        extended.at[pl.ds(pl.multiple_of(node_count + me_d * cap, cap), cap), :],
    )
    own_cols = rows(me_m, share)
    across_cols = rows(across, share)

    def weight_first(weight, whole):
        half = rows(me_g, weight.shape[0] // 2)
        return [
            put({"mp": across}, weight.at[half, :], whole.at[half, own_cols]),
            put({"mp": mate}, weight, whole.at[:, own_cols]),
        ]

    def weight_second(first, whole):
        first[0].wait_recv()
        part = whole.at[rows(me_g, whole.shape[0] // 2), across_cols]
        return first[1:] + [
            put({"groups": 1 - me_g}, part, part),
            put({"mp": mate}, part, part),
        ]

    def weight_third(second, whole):
        second[1].wait_recv()
        part = whole.at[rows(1 - me_g, whole.shape[0] // 2), across_cols]
        return [second[0], second[2], put({"mp": mate}, part, part)]

    w_out_in = weight_first(w_out, w_out_all)
    nw_in_in = weight_first(nw_in, nw_in_all)
    nw_out_in = weight_first(nw_out, nw_out_all)
    gain_in = push("mp", 1, mp_to, lambda peer: e_gain, e_gain_all.at[:, own_cols])
    ngain_in = push("mp", 2, mp_to, lambda peer: n_gain, n_gain_all.at[:, own_cols])
    ncot_in = push(
        "mp", 3, mp_to, lambda peer: node_cot.at[rows(peer, my_nodes), :], ncot_rows.at[:, own_cols]
    )
    w_out_all[:, own_cols] = w_out[...]
    e_gain_all[:, own_cols] = e_gain[...]
    n_gain_all[:, own_cols] = n_gain[...]
    ncot_rows[:, own_cols] = node_cot[rows(me_m, my_nodes), :]
    nw_in_all[:, own_cols] = nw_in[...]
    nw_out_all[:, own_cols] = nw_out[...]
    w_in_rows[:, :, own_cols] = w_in[:, rows(me_m, share), :]

    lane = 128
    before = (
        lax.broadcasted_iota(jnp.int32, (lane, lane), 0)
        < lax.broadcasted_iota(jnp.int32, (lane, lane), 1)
    ).astype(bf16)
    offset = jnp.zeros((node_count, 1), f32)
    places = []
    for start in range(0, edge_count, lane):
        received = receivers[:, start : start + lane]
        hot = lax.broadcasted_iota(jnp.int32, (node_count, lane), 0) == received
        hot32 = hot.astype(f32)
        earlier = dot_plain(hot32.astype(bf16), before) + offset
        rank = jnp.sum(hot32 * earlier, axis=0, keepdims=True)
        places.append(received * degree + rank.astype(jnp.int32))
        offset = offset + jnp.sum(hot32, axis=1, keepdims=True)
    place = jnp.concatenate(places, axis=1)
    sender_cols = (
        lax.broadcasted_iota(jnp.int32, (node_count + slots, edge_count), 0) == senders[...]
    ).astype(bf16)
    receiver_pre[...] = dot_plain(nodes[...], w_in[2])
    owners = [across, across_mate, mate, me_m]
    cot_in = []
    for step, owner in enumerate(owners):
        block = rows(owner, my_edges)
        hot = (
            lax.broadcasted_iota(jnp.int32, (my_edges, edge_count), 0) + owner * my_edges == place
        ).astype(bf16)
        perm[block, :] = hot
        cot_sorted[block, :] = dot_plain(hot, edge_cot[...]).astype(bf16)
        if step < mp - 1:
            cot_in.append(put({"mp": owner}, cot_sorted.at[block, :], cot_rows.at[:, own_cols]))
        edges_sorted[block, :] = dot_plain(hot, edges[...]).astype(bf16)
        sender_hot[block, :] = dot_last(hot, sender_cols).astype(bf16)
        if step == mp // 2:
            w_out_in = weight_second(w_out_in, w_out_all)
    nw_in_in = weight_second(nw_in_in, nw_in_all)
    nw_out_in = weight_second(nw_out_in, nw_out_all)
    arrived(halo)
    sender_pre = two_terms(dot_plain(extended[...], w_in[1]))
    pre_in = []
    for step, owner in enumerate(owners):
        block = rows(owner, my_edges)
        local = dot_plain(edges_sorted[block, :], w_in[0])
        local = local + repeat_rows(receiver_pre[rows(owner, my_nodes), :], degree)
        local = local + join_terms(dot_plain(sender_hot[block, :], sender_pre))
        pre_cols[block, :] = local.astype(bf16)
        if step < mp - 1:
            pre_in.append(put({"mp": owner}, pre_cols.at[block, :], pre_rows.at[:, own_cols]))
    pre_rows[:, own_cols] = pre_cols[rows(me_m, my_edges), :]
    cot_rows[:, own_cols] = cot_sorted[rows(me_m, my_edges), :]

    w_out_in = weight_third(w_out_in, w_out_all)
    arrived(pre_in)
    w_in_in = push(
        "mp", 8, mp_to, lambda peer: w_in.at[:, rows(peer, share), :], w_in_rows.at[:, :, own_cols]
    )
    edge_pre = pre_rows[...].astype(f32)
    edge_hidden = (edge_pre * jax.nn.sigmoid(edge_pre)).astype(bf16)
    arrived(w_out_in)
    edge_out = dot_plain(edge_hidden, w_out_all[...])
    edge_hat, edge_rstd = local_norm(edge_out)
    arrived(gain_in)
    edge_update = (edge_hat * e_gain_all[...]).astype(bf16).astype(f32)
    own_rows = rows(me_m, my_nodes)
    aggregate = sum_rows(edge_update, degree).astype(bf16)
    agg_all[own_rows, :] = aggregate
    agg_in = push(
        "mp", 9, mp_to, lambda peer: agg_all.at[own_rows, :], agg_all.at[own_rows, :]
    )
    nw_in_in = weight_third(nw_in_in, nw_in_all)
    nw_out_in = weight_third(nw_out_in, nw_out_all)
    arrived(nw_in_in)
    node_pre = dot_plain(nodes[own_rows, :], nw_in_all[pl.ds(0, width), :]) + dot_plain(
        aggregate, nw_in_all[pl.ds(width, width), :]
    )
    node_hidden = (node_pre * jax.nn.sigmoid(node_pre)).astype(bf16)
    nhid_all[own_rows, :] = node_hidden
    nhid_in = push(
        "mp", 10, mp_to, lambda peer: nhid_all.at[own_rows, :], nhid_all.at[own_rows, :]
    )
    arrived(nw_out_in)
    node_hat, node_rstd = local_norm(dot_plain(node_hidden, nw_out_all[...]))
    arrived(ncot_in)
    arrived(ngain_in)
    ncot = ncot_rows[...].astype(f32)
    gain_part[...] = jnp.zeros_like(gain_part)
    gain_part[0:1, :] = jnp.sum(ncot * node_hat, axis=0, keepdims=True) * node_scale
    node_slope = local_norm_back(ncot, n_gain_all[...], node_hat, node_rstd).astype(bf16)
    nslope_own[...] = node_slope
    nslope_in = push(
        "mp", 11, mp_to, lambda peer: nslope_own.at[:, rows(peer, share)], nslope_cols.at[own_rows, :]
    )
    nslope_cols[own_rows, :] = nslope_own[:, own_cols]
    node_delta = (dot_last(node_slope, nw_out_all[...]) * silu_slope(node_pre)).astype(bf16)
    ndelta_all[own_rows, :] = node_delta
    ndelta_in = push(
        "mp", 12, mp_to, lambda peer: ndelta_all.at[own_rows, :], ndelta_all.at[own_rows, :]
    )
    agg_back = dot_last(node_delta, nw_in_all[pl.ds(width, width), :])
    arrived(cot_in)
    update_grad = cot_rows[...].astype(f32) + repeat_rows(agg_back, degree)
    gain_part[1:2, :] = jnp.sum(update_grad * edge_hat, axis=0, keepdims=True) * edge_scale
    edge_slope = local_norm_back(update_grad, e_gain_all[...], edge_hat, edge_rstd).astype(bf16)
    edge_pre = pre_rows[...].astype(f32)
    edge_delta = (dot_last(edge_slope, w_out_all[...]) * silu_slope(edge_pre)).astype(bf16)
    own_edges = rows(me_m, my_edges)
    delta_all[own_edges, :] = edge_delta
    cols = [rows(owner, share) for owner in owners]

    def delta_piece(device, owner, col):
        piece = delta_all.at[rows(owner, my_edges), col]
        return put({"mp": device}, piece, piece)

    delta_own_cols = [delta_piece(across, me_m, cols[0]), delta_piece(across_mate, me_m, cols[1])]
    own_delta = delta_all.at[own_edges, :]
    delta_mate = put({"mp": mate}, own_delta, own_delta)
    eo_part[...] = (dot_first(edge_hidden, edge_slope) * edge_scale).astype(bf16)
    eo_in = [
        put({"mp": mate}, eo_part.at[:, rows(mate, share)], eo_recv.at[0]),
        put({"mp": mate}, eo_part.at[:, rows(across_mate, share)], eo_recv.at[1]),
    ]
    delta_rest = [delta_piece(across, me_m, col) for col in cols[1:]]
    gain_part_in = push(
        "mp", 15, mp_to, lambda peer: gain_part.at[:, rows(peer, share)], gain_recv.at[me_m]
    )
    gain_recv[me_m] = gain_part[:, own_cols]

    arrived(agg_in)
    arrived(nhid_in)
    arrived(nslope_in)
    arrived(ndelta_in)
    no_send[...] = (dot_first(nhid_all[...], nslope_cols[...]) * node_scale).astype(bf16)
    ndelta_cols = ndelta_all[:, own_cols]
    ni_send[pl.ds(0, width), :] = (dot_first(nodes[...], ndelta_cols) * node_scale).astype(bf16)
    ni_send[pl.ds(width, width), :] = (dot_first(agg_all[...], ndelta_cols) * node_scale).astype(
        bf16
    )

    def scatter_sum(kind, parts, landed):
        size = landed.shape[1]
        copies = push(
            "dom", kind, dom_to, lambda peer: parts.at[rows(peer, size), :], landed.at[me_d]
        )
        landed[me_d] = parts[rows(me_d, size), :]
        return copies

    no_in = scatter_sum(1, no_send, no_dom)
    ni_in = scatter_sum(2, ni_send, ni_dom)
    total = node_cot[...].astype(f32) + dot_last(ndelta_all[...], nw_in_all[own_cols, :])

    delta_mate.wait_recv()
    arrived(delta_own_cols)
    delta_cols = delta_all[:, own_cols]
    own_scale = jnp.float32(edge_scale)
    ei_send[pl.ds(0, width), :] = (dot_first(edges_sorted[...], delta_cols) * own_scale).astype(
        bf16
    )
    by_sender = two_terms(dot_first(sender_hot[...], delta_cols))
    ei_send[pl.ds(width, width), :] = (
        join_terms(dot_first(extended[...], by_sender)) * own_scale
    ).astype(bf16)
    by_receiver = two_terms(sum_rows(delta_cols.astype(f32), degree))
    ei_send[pl.ds(2 * width, width), :] = (
        join_terms(dot_first(nodes[...], by_receiver)) * own_scale
    ).astype(bf16)
    ei_in = scatter_sum(4, ei_send, ei_dom)
    arrived(eo_in)
    eo_recv[2] = (eo_part[:, across_cols].astype(f32) + eo_recv[1].astype(f32)).astype(bf16)
    eo_across = put({"mp": across}, eo_recv.at[2], eo_recv.at[3])

    arrived(w_in_in)

    def input_back(owner):
        block = rows(owner, my_edges)
        deltas = delta_all[block, :]
        grad = cot_sorted[block, :].astype(f32) + dot_last(deltas, w_in_rows[0])
        grad_sorted[block, :] = grad.astype(bf16)
        back_terms[block, :] = two_terms(dot_last(deltas, w_in_rows[1]))
        receiver_back[rows(owner, my_nodes), :] = sum_rows(
            dot_last(deltas, w_in_rows[2]), degree
        )

    input_back(me_m)
    input_back(mate)
    arrived(delta_rest)
    delta_last = [delta_piece(mate, across, col) for col in (cols[3], cols[0], cols[1])]
    eo_across.wait_recv()
    eo_send[...] = (
        eo_part[:, own_cols].astype(f32) + eo_recv[0].astype(f32) + eo_recv[3].astype(f32)
    ).astype(bf16)
    eo_out = scatter_sum(5, eo_send, eo_dom)
    input_back(across)
    arrived(delta_last)
    input_back(across_mate)
    sender_sums = join_terms(dot_first(sender_hot[...], back_terms[...]))
    cross_send[...] = sender_sums[node_count:].astype(bf16)
    cross_recv[rows(me_d, cap), :] = jnp.zeros((cap, share), bf16)
    cross_in = push(
        "dom",
        3,
        dom_to,
        lambda peer: cross_send.at[rows(peer, cap), :],
        cross_recv.at[rows(me_d, cap), :],
    )
    arrived(gain_part_in)
    gain_sum[...] = jnp.sum(gain_recv[...], axis=0)
    gain_out = push("dom", 6, dom_to, lambda peer: gain_sum, gain_dom.at[me_d])
    gain_dom[me_d] = gain_sum[...]

    edge_grad[...] = dot_first(perm[...], grad_sorted[...]).astype(bf16)
    arrived(no_in)
    node_out_grad[...] = jnp.sum(no_dom[...].astype(f32), axis=0)
    arrived(ni_in)
    node_in_grad[...] = jnp.sum(ni_dom[...].astype(f32), axis=0)
    arrived(cross_in)
    node_grad[...] = (
        total + receiver_back[...] + sender_sums[:node_count] + dot_plain(table_hot, cross_recv[...])
    ).astype(bf16)
    arrived(gain_out)
    gains = jnp.sum(gain_dom[...], axis=0)
    node_gain_grad[...] = gains[0:1]
    edge_gain_grad[...] = gains[1:2]
    arrived(eo_out)
    edge_out_grad[...] = jnp.sum(eo_dom[...].astype(f32), axis=0)
    arrived(ei_in)
    edge_in_grad[...] = jnp.sum(ei_dom[...].astype(f32), axis=0)
    for copy in started:
        copy.wait_send()


def fits_kernel(mesh):
    return mesh.shape["groups"] == 2 and mesh.shape["mp"] == 4 and mesh.shape["dom"] <= 8


def hand_over_kernel(*refs):
    count = len(refs) // 2
    for source, target in zip(refs[:count], refs[count:]):
        target[...] = source[...]


def fused_body(
    node_latents,
    edge_latents,
    node_cotangent,
    edge_cotangent,
    senders,
    receivers,
    send_nodes,
    edge_in_weight,
    edge_out_weight,
    edge_gain,
    node_in_weight,
    node_out_weight,
    node_gain,
):
    dom, mp = lax.axis_size("dom"), lax.axis_size("mp")
    node_count, width = node_latents.shape
    edge_count = edge_latents.shape[0]
    slots = send_nodes.shape[1] * send_nodes.shape[2]
    share = width // mp
    my_nodes, my_edges = node_count // mp, edge_count // mp
    f32, bf16 = jnp.float32, jnp.bfloat16
    shape = jax.ShapeDtypeStruct
    outs = (
        shape((node_count, share), bf16),
        shape((edge_count, share), bf16),
        shape((3 * width // dom, share), f32),
        shape((width // dom, share), f32),
        shape((1, share), f32),
        shape((2 * width // dom, share), f32),
        shape((width // dom, share), f32),
        shape((1, share), f32),
    )
    scratch = [
        ((slots, width), bf16),
        ((node_count + slots, width), bf16),
        ((width, width), bf16),
        ((2 * width, width), bf16),
        ((width, width), bf16),
        ((3, share, width), bf16),
        ((1, width), f32),
        ((1, width), f32),
        ((edge_count, edge_count), bf16),
        ((edge_count, width), bf16),
        ((edge_count, share), bf16),
        ((edge_count, share), bf16),
        ((edge_count, node_count + slots), bf16),
        ((edge_count, share), bf16),
        ((my_edges, width), bf16),
        ((my_edges, width), bf16),
        ((my_nodes, width), bf16),
        ((node_count, width), bf16),
        ((node_count, width), bf16),
        ((node_count, width), bf16),
        ((my_nodes, width), bf16),
        ((node_count, share), bf16),
        ((edge_count, width), bf16),
        ((8, width), f32),
        ((mp, 8, share), f32),
        ((8, share), f32),
        ((dom, 8, share), f32),
        ((width, width), bf16),
        ((mp, width, share), bf16),
        ((width, share), bf16),
        ((dom, width // dom, share), bf16),
        ((3 * width, share), bf16),
        ((dom, 3 * width // dom, share), bf16),
        ((width, share), bf16),
        ((dom, width // dom, share), bf16),
        ((2 * width, share), bf16),
        ((dom, 2 * width // dom, share), bf16),
        ((slots, share), bf16),
        ((slots, share), bf16),
        ((edge_count, 2 * share), bf16),
        ((node_count, share), f32),
        ((node_count, share), f32),
    ]
    vmem = pl.BlockSpec(memory_space=pltpu.VMEM)
    results = pl.pallas_call(
        functools.partial(fused_kernel, dom, mp, edge_count // node_count),
        out_shape=outs,
        in_specs=[vmem] * 13,
        out_specs=tuple([vmem] * 8),
        scratch_shapes=[pltpu.VMEM(dims, kind) for dims, kind in scratch]
        + [
            pltpu.SemaphoreType.DMA((16, mp - 1)),
            pltpu.SemaphoreType.DMA((16, mp - 1)),
            pltpu.SemaphoreType.DMA((7, dom - 1)),
            pltpu.SemaphoreType.DMA((7, dom - 1)),
            pltpu.SemaphoreType.DMA((40,)),
            pltpu.SemaphoreType.DMA((40,)),
        ],
        compiler_params=pltpu.CompilerParams(
            collective_id=0, has_side_effects=True, vmem_limit_bytes=56 * 1024 * 1024
        ),
        name="layer_backward",
    )(
        node_latents,
        edge_latents,
        node_cotangent,
        edge_cotangent,
        senders.reshape(1, edge_count),
        receivers.reshape(1, edge_count),
        send_nodes.reshape(send_nodes.shape[1:]),
        edge_in_weight.reshape(3, width, share),
        edge_out_weight,
        edge_gain.reshape(1, share),
        node_in_weight,
        node_out_weight,
        node_gain.reshape(1, share),
    )
    results = list(
        pl.pallas_call(
            hand_over_kernel,
            out_shape=outs,
            in_specs=[vmem] * len(outs),
            out_specs=tuple([vmem] * len(outs)),
            name="hand_over",
        )(*results)
    )
    results[4], results[7] = results[4].reshape(share), results[7].reshape(share)
    return tuple(results)


def solution(mesh):
    in_specs = (
        P(("groups", "dom"), None),
        P(("groups", "dom"), None),
        P(("groups", "dom"), "mp"),
        P(("groups", "dom"), "mp"),
        P("dom"),
        P("dom"),
        P("dom", None, None),
        P(None, "mp"),
        P(None, "mp"),
        P("mp"),
        P(None, "mp"),
        P(None, "mp"),
        P("mp"),
    )
    out_specs = (
        P(("groups", "dom"), "mp"),
        P(("groups", "dom"), "mp"),
        P(("groups", "dom"), "mp"),
        P(("groups", "dom"), "mp"),
        P(("groups", "mp")),
        P(("groups", "dom"), "mp"),
        P(("groups", "dom"), "mp"),
        P(("groups", "mp")),
    )
    return jax.shard_map(fused_body if fits_kernel(mesh) else body, mesh=mesh, in_specs=in_specs, out_specs=out_specs, check_vma=False)
```
